32 devices in a mesh: seg: 8 (over y, x, core), coil: 4 (over z).
Axes of the slice: x: 2, y: 2, z: 4, core: 2. Of those that a mesh axis runs over, the one named last changes fastest.
Arguments:
- measured: float32 [16, 2, 32, 8, 512], P('seg', None, 'coil'), may hold values from -0.4 to 0.4
- forward_kernel: float32 [16, 2, 256, 128], P('seg', None, None, 'coil'), may hold values from -0.375 to 0.375
- backward_kernel: float32 [16, 2, 256, 128], P('seg', None, None, 'coil'), may hold values from -0.375 to 0.375
- line_offsets: int32 [16, 2, 4], P('seg'), may hold values from 0 to 7
Outputs:
- forward: float32 [16, 2, 32, 8, 512], P('seg', None, 'coil')
- result: float32 [16, 2, 32, 8, 512], P('seg', None, 'coil')
The draws below stay inside these ranges and needn't reach their ends.
All inputs are finite; a program needn't handle non-finite values.
Results may differ from the reference program's by a relative error of at most 0.0003.
Values sent between devices are 32-bit elements; how exact they have to be, the bound alone decides.
No kernel may reach another device: no remote copies, remote signals or barrier semaphores. Data moves between devices by JAX's collectives and lax.ppermute only.
A program may use at most 128 MiB of HBM per device.

```python
import jax
import jax.numpy as jnp
from jax import lax

COILS = 32
X = 512
LINES = 8
J = 4
SEGS = 16
STATE = 512


def with_ends(values, key, least, high):
    longest = values.shape.index(max(values.shape))
    spots = []
    for shift in (0, 1):
        where = [jax.random.randint(jax.random.fold_in(key, axis), (), 0, length) for axis, length in enumerate(values.shape)]
        where[longest] = (where[longest] + shift) % values.shape[longest]
        spots.append(tuple(where))
    return values.at[spots[0]].set(least).at[spots[1]].set(high)


def steps_of(key, shape, pieces, low, top_value):
    level = 1.0
    for dim, blocks in pieces:
        heights = jax.random.uniform(jax.random.fold_in(jax.random.fold_in(key, 6), dim), (blocks,), jnp.float32, low / len(pieces), top_value / len(pieces))
        level = level * jnp.repeat(jnp.exp(heights), shape[dim] // blocks).reshape((-1,) + (1,) * (len(shape) - 1 - dim))
    return level


def centred(own_key, dims, scale, limit, cuts=(), held_as=jnp.bfloat16):
    level = steps_of(own_key, dims, cuts, -0.22, 0.18) if cuts else 1.0
    values = jax.random.normal(own_key, dims, jnp.float32) * scale * level
    return jnp.minimum(jnp.maximum(values, -limit), limit).astype(held_as)


def setup_inputs(seed: int = 0) -> dict:
    keys = jax.random.split(jax.random.key(seed), 5)
    measured = centred(keys[0], (SEGS, 2, COILS, LINES, X), 0.05, 0.4, ((0, 8), (2, 4)), jnp.float32)
    forward_kernel = centred(keys[1], (SEGS, 2, COILS * LINES, COILS * J), (2 * COILS * J) ** -0.5, 0.375, ((0, 8), (3, 4)), jnp.float32)
    backward_kernel = centred(keys[2], (SEGS, 2, COILS * LINES, COILS * J), (2 * COILS * J) ** -0.5, 0.375, ((0, 8), (3, 4)), jnp.float32)
    line_offsets = with_ends(jax.random.randint(keys[3], (SEGS, 2, J), 0, LINES), jax.random.fold_in(keys[3], 1), 0, LINES - 1).astype(jnp.int32)
    return {"measured": measured, "forward_kernel": forward_kernel, "backward_kernel": backward_kernel, "line_offsets": line_offsets}


PRECISE = lax.Precision.HIGHEST


def build_maps(kernel, offsets):
    blocks = kernel.shape[0]
    source_taps = offsets.shape[1]
    coil_count = kernel.shape[3] // source_taps
    line_count = kernel.shape[2] // coil_count
    line_picks = (offsets[:, :, None] == jnp.arange(line_count, dtype=jnp.int32)[None, None, :]).astype(jnp.float32)
    kernel_parts = kernel.astype(jnp.float32).reshape(blocks, 2, coil_count * line_count, coil_count, source_taps)
    spread = jnp.einsum("srocj,sjl->srocl", kernel_parts, line_picks, precision=PRECISE)
    spread = spread.reshape(blocks, 2, coil_count * line_count, coil_count * line_count)
    upper_rows = jnp.concatenate([spread[:, 0], -spread[:, 1]], axis=2)
    lower_rows = jnp.concatenate([spread[:, 1], spread[:, 0]], axis=2)
    return jnp.concatenate([upper_rows, lower_rows], axis=1)


def sweep(seg_maps, sources, backward):
    def advance(carried, inputs):
        matrix, source = inputs
        updated = jnp.dot(matrix, carried, precision=PRECISE) + source
        return updated, updated
    initial = jnp.zeros(sources.shape[1:], jnp.float32)
    _, states = lax.scan(advance, initial, (seg_maps, sources), reverse=backward)
    return states


def reference(measured, forward_kernel, backward_kernel, line_offsets):
    sources = measured.reshape(SEGS, STATE, X)
    forward = sweep(build_maps(forward_kernel, line_offsets[:, 0]), sources, False)
    result = sweep(build_maps(backward_kernel, line_offsets[:, 1]), forward, True)
    return forward.reshape(measured.shape), result.reshape(measured.shape)
```

```python
import functools

import jax
import jax.numpy as jnp
from jax import lax
from jax.experimental import pallas as pl
from jax.experimental.pallas import tpu as pltpu
from jax.sharding import PartitionSpec as P

F32 = jnp.float32
BF16 = jnp.bfloat16
VMEM = pl.BlockSpec(memory_space=pltpu.VMEM)
SMEM = pl.BlockSpec(memory_space=pltpu.SMEM)
ANY = pl.BlockSpec(memory_space=pl.ANY)
LANES = 128
PARAMS = pltpu.CompilerParams(vmem_limit_bytes=40 * 2**20)


def halves(a):
    high = a.astype(BF16)
    return high, (a - high.astype(F32)).astype(BF16)


def product(left, right):
    dot = functools.partial(jnp.dot, preferred_element_type=F32)
    high, low = left
    other_high, other_low = halves(right)
    return dot(high, other_high) + (dot(high, other_low) + dot(low, other_high))


def real_form(columns):
    size = columns.shape[0] // 2
    return jnp.concatenate([columns, jnp.concatenate([-columns[size:], columns[:size]], axis=0)], axis=1)


def spread(value):
    return [value[:, i : i + LANES] for i in range(0, value.shape[1], LANES)]


def pick(value, state, picked, offsets, row, coils, lines):
    taps = offsets.shape[1]
    chunks = spread(value)
    for i, chunk in enumerate(chunks):
        state[i] = chunk
        for part in range(2):
            for tap in range(taps):
                source = pl.ds(part * coils * lines + offsets[row, tap], coils, stride=lines)
                picked[i, pl.ds(part * coils * taps + tap, coils, stride=taps), :] = state[i, source, :]
    return jnp.concatenate([picked[i] for i in range(len(chunks))], axis=1)


def spot(ids, i):
    return lax.bitwise_xor(ids[0], i)


def pack(measured, kernels_f, kernels_b, ids):
    segs, parts, coils, lines, samples = measured.shape
    n = lax.axis_size("coil")
    width = samples // n
    cols, rows = kernels_f.shape[2:]

    def body(ids_ref, m_ref, f_ref, b_ref, k_out, *rest):
        outs, sems = rest[:n], rest[n]
        copies = [
            pltpu.make_async_copy(f_ref, k_out.at[pl.ds(0, segs)], sems.at[n]),
            pltpu.make_async_copy(b_ref, k_out.at[pl.ds(segs, segs)], sems.at[n + 1]),
        ]
        for i in range(n):
            start = pl.multiple_of(spot(ids_ref, i) * width, width)
            copies.append(pltpu.make_async_copy(m_ref.at[:, :, :, :, pl.ds(start, width)], outs[i], sems.at[i]))
        for c in copies:
            c.start()
        for c in copies:
            c.wait()

    return pl.pallas_call(
        body,
        out_shape=[jax.ShapeDtypeStruct((2 * segs, parts, cols, rows), F32)]
        + [jax.ShapeDtypeStruct((segs, parts, coils, lines, width), F32)] * n,
        in_specs=[SMEM, ANY, ANY, ANY],
        out_specs=[VMEM] * (n + 1),
        scratch_shapes=[pltpu.SemaphoreType.DMA((n + 2,))],
        compiler_params=PARAMS,
        name="pack",
    )(ids, measured, kernels_f, kernels_b)


def summary(ids, offsets, kernel_blocks, lines_blocks, taps):
    n = len(kernel_blocks)
    maps, _, block_cols, rows = kernel_blocks[0].shape
    own_coils = block_cols // taps
    coils = own_coils * n
    lines = rows // coils
    cols = block_cols * n
    segs, _, _, _, width = lines_blocks[0].shape
    size = 2 * cols

    def body(ids_ref, off_ref, *refs):
        k_refs, m_refs = refs[:n], refs[n : 2 * n]
        e_ref, hi_ref, lo_ref, m_ref = refs[2 * n : 2 * n + 4]
        kt, state, picked = refs[2 * n + 4 :]
        choose = functools.partial(pick, state=state, picked=picked, offsets=off_ref, coils=coils, lines=lines)
        for i in range(n):
            r = spot(ids_ref, i)
            m_ref[:, :, pl.ds(r * own_coils, own_coils)] = m_refs[i][...]
            kt[:, :, pl.ds(r, 1)] = k_refs[i][...][:, :, None]
        columns = []
        for k in range(maps):
            real, imag = (kt[k, part].reshape(cols, rows).T for part in range(2))
            columns.append(jnp.concatenate([real, imag], axis=0))
            hi_ref[k], lo_ref[k] = halves(real_form(columns[k]))
        m = [m_ref[s].reshape(2 * rows, width) for s in range(segs)]
        first = jnp.concatenate([columns[0], m[0]], axis=1)
        stepped = product((hi_ref[1], lo_ref[1]), choose(first, row=1))
        second = jnp.concatenate([stepped[:, :cols], stepped[:, cols:] + m[1]], axis=1)
        e_ref[:, : cols + width] = choose(second, row=4)
        third = jnp.concatenate([second, columns[3]], axis=1)
        stepped = product((hi_ref[2], lo_ref[2]), choose(third, row=2))
        last = jnp.concatenate([stepped[:, : cols + width] + first, stepped[:, cols + width :]], axis=1)
        e_ref[:, cols + width :] = choose(last, row=5)

    return pl.pallas_call(
        body,
        out_shape=[
            jax.ShapeDtypeStruct((size, 3 * cols + 2 * width), F32),
            jax.ShapeDtypeStruct((maps, 2 * rows, size), BF16),
            jax.ShapeDtypeStruct((maps, 2 * rows, size), BF16),
            jax.ShapeDtypeStruct((segs, 2, coils, lines, width), F32),
        ],
        in_specs=[SMEM, SMEM] + [VMEM] * (2 * n),
        out_specs=[VMEM] * 4,
        scratch_shapes=[
            pltpu.VMEM((maps, 2, n, block_cols, rows), F32),
            pltpu.VMEM(((2 * cols + width) // LANES, 2 * rows, LANES), F32),
            pltpu.VMEM(((2 * cols + width) // LANES, size, LANES), F32),
        ],
        compiler_params=PARAMS,
        name="summary",
    )(ids, offsets, *kernel_blocks, *lines_blocks)


def compose(ids, mine, other, cols):
    size, lanes = mine.shape
    width = (lanes - 3 * cols) // 2
    half = cols + width

    def body(ids_ref, a_ref, b_ref, out_ref, pair, whole):
        core = ids_ref[2]
        pair[pl.ds(core, 1)] = a_ref[...][None]
        pair[pl.ds(1 - core, 1)] = b_ref[...][None]
        a, b = pair[0], pair[1]
        forward = halves(real_form(b[:, :cols]))
        cross = halves(real_form(b[:, half : half + cols]))
        back = halves(real_form(a[:, 2 * half :]))
        head = product(forward, a[:, :half])
        inner = product(cross, a[:, :half])
        whole[:, :cols] = head[:, :cols]
        whole[:, cols:half] = head[:, cols:] + b[:, cols:half]
        right = jnp.concatenate([inner[:, :cols], inner[:, cols:] + b[:, half + cols : 2 * half], b[:, 2 * half :]], axis=1)
        tail = product(back, right)
        whole[:, half : 2 * half] = tail[:, :half] + a[:, half : 2 * half]
        whole[:, 2 * half :] = tail[:, half:]
        out_ref[...] = whole[pl.ds(pl.multiple_of(core * (size // 2), size // 2), size // 2), :]

    return pl.pallas_call(
        body,
        out_shape=jax.ShapeDtypeStruct((size // 2, lanes), F32),
        in_specs=[SMEM, VMEM, VMEM],
        out_specs=VMEM,
        scratch_shapes=[pltpu.VMEM((2, size, lanes), F32), pltpu.VMEM((size, lanes), F32)],
        compiler_params=PARAMS,
        name="compose",
    )(ids, mine, other)


def finish(ids, offsets, high, low, measured, mine, other, near, far):
    maps, state_size, size = high.shape
    segs, _, coils, lines, width = measured.shape
    cols = size // 2
    half = cols + width
    lanes = mine.shape[1]
    chips = len(near)
    n = lax.axis_size("coil")
    own_coils = coils // n

    def body(ids_ref, off_ref, hi_ref, lo_ref, m_ref, a_ref, b_ref, *refs):
        near_refs, far_refs = refs[:chips], refs[chips : 2 * chips]
        outs = refs[2 * chips : 2 * chips + n]
        pair, table, zs, ws, state, picked, states = refs[2 * chips + n :]
        chip, core = ids_ref[1], ids_ref[2]
        pair[pl.ds(core, 1)] = a_ref[...][None]
        pair[pl.ds(1 - core, 1)] = b_ref[...][None]
        for i in range(chips):
            e = lax.bitwise_xor(chip, i)
            table[pl.ds(e * 2 + core, 1)] = near_refs[i][...][None]
            table[pl.ds(e * 2 + 1 - core, 1)] = far_refs[i][...][None]

        def block(e, start, stop):
            return jnp.concatenate([table[2 * e, :, start:stop], table[2 * e + 1, :, start:stop]], axis=0)

        def matrix(columns):
            return halves(real_form(columns))

        zs[0] = jnp.zeros((size, width), F32)
        z = None
        for e in range(chips - 1):
            incoming = block(e, cols, half)
            z = incoming if z is None else product(matrix(block(e, 0, cols)), z) + incoming
            zs[e + 1] = z
        ws[chips - 1] = jnp.zeros((size, width), F32)
        w = None
        for e in range(chips - 1, 0, -1):
            local = product(matrix(block(e, half, half + cols)), zs[e]) + block(e, half + cols, 2 * half)
            w = local if w is None else product(matrix(block(e, 2 * half, lanes)), w) + local
            ws[e - 1] = w
        zc, wc = zs[chip], ws[chip]
        z_mid = product(matrix(pair[0, :, :cols]), zc) + pair[0, :, cols:half]
        w_mid = (
            product(matrix(pair[1, :, 2 * half :]), wc)
            + product(matrix(pair[1, :, half : half + cols]), z_mid)
            + pair[1, :, half + cols : 2 * half]
        )
        first_core = core == 0
        z = jnp.where(first_core, zc, z_mid)
        w = jnp.where(first_core, w_mid, wc)
        m = [m_ref[s].reshape(state_size, width) for s in range(segs)]
        f0 = product((hi_ref[0], lo_ref[0]), z) + m[0]
        choose = functools.partial(pick, state=state, picked=picked, offsets=off_ref, coils=coils, lines=lines)
        f1 = product((hi_ref[1], lo_ref[1]), choose(f0, row=1)) + m[1]
        r1 = product((hi_ref[3], lo_ref[3]), w) + f1
        r0 = product((hi_ref[2], lo_ref[2]), choose(r1, row=2)) + f0
        for i, value in enumerate((f0, f1, r0, r1)):
            states[i // segs, i % segs] = value.reshape(2, coils, lines, width)
        for i in range(n):
            outs[i][...] = states[:, :, :, pl.ds(spot(ids_ref, i) * own_coils, own_coils)]

    return pl.pallas_call(
        body,
        out_shape=[jax.ShapeDtypeStruct((2, segs, 2, own_coils, lines, width), F32)] * n,
        in_specs=[SMEM, SMEM] + [VMEM] * (5 + 2 * chips),
        out_specs=[VMEM] * n,
        scratch_shapes=[
            pltpu.VMEM((2, size, lanes), F32),
            pltpu.VMEM((2 * chips, size // 2, lanes), F32),
            pltpu.VMEM((chips, size, width), F32),
            pltpu.VMEM((chips, size, width), F32),
            pltpu.VMEM((width // LANES, state_size, LANES), F32),
            pltpu.VMEM((width // LANES, size, LANES), F32),
            pltpu.VMEM((2, segs, 2, coils, lines, width), F32),
        ],
        compiler_params=PARAMS,
        name="finish",
    )(ids, offsets, high, low, measured, mine, other, *near, *far)


def unpack(blocks, ids):
    n = len(blocks)
    _, segs, parts, coils, lines, width = blocks[0].shape

    def body(ids_ref, *refs):
        ins, outs, sems = refs[:n], refs[n : n + 2], refs[n + 2]
        copies = []
        for i in range(n):
            start = pl.multiple_of(spot(ids_ref, i) * width, width)
            for o in range(2):
                copies.append(pltpu.make_async_copy(ins[i].at[o], outs[o].at[:, :, :, :, pl.ds(start, width)], sems.at[i, o]))
        for c in copies:
            c.start()
        for c in copies:
            c.wait()

    return pl.pallas_call(
        body,
        out_shape=[jax.ShapeDtypeStruct((segs, parts, coils, lines, n * width), F32)] * 2,
        in_specs=[SMEM] + [VMEM] * n,
        out_specs=[ANY] * 2,
        scratch_shapes=[pltpu.SemaphoreType.DMA((n, 2))],
        compiler_params=PARAMS,
        name="unpack",
    )(ids, *blocks)


def swap(block, axis, distance):
    return lax.ppermute(block, axis, [(i, i ^ distance) for i in range(lax.axis_size(axis))])


def shards(measured, forward_kernel, backward_kernel, line_offsets):
    n = lax.axis_size("coil")
    places = lax.axis_size("seg")
    coil, seg = lax.axis_index("coil"), lax.axis_index("seg")
    chips = places // 2
    taps = line_offsets.shape[2]
    width = measured.shape[4] // n
    cols = forward_kernel.shape[3] * n
    ids = jnp.stack([coil, seg // 2, seg % 2]).astype(jnp.int32)
    after = lax.ppermute(line_offsets[0, 0], "seg", [(i + 1, i) for i in range(places - 1)])
    before = lax.ppermute(line_offsets[-1, 1], "seg", [(i, i + 1) for i in range(places - 1)])
    offsets = jnp.concatenate([line_offsets[:, 0], line_offsets[:, 1], after[None], before[None]])
    kernels_f, kernels_b = (jnp.swapaxes(k, 2, 3) for k in (forward_kernel, backward_kernel))
    if width % LANES == 0 and (cols // taps // n) % 8 == 0:
        packed = pack(measured, kernels_f, kernels_b, ids)
        own, pieces = packed[0], packed[1:]
        kernel_blocks = {0: own}
        distance = n // 2
        while distance:
            held = sorted(kernel_blocks)
            received = swap(jnp.stack([kernel_blocks[i] for i in held]), "coil", distance)
            for at, i in enumerate(held):
                kernel_blocks[i ^ distance] = received[at]
            distance //= 2
        kernel_blocks = [kernel_blocks[i] for i in range(n)]
        lines_blocks = [pieces[0]] + [swap(pieces[i], "coil", i) for i in range(1, n)]
        order = ids
    else:
        whole = lax.all_gather(jnp.concatenate([kernels_f, kernels_b]), "coil")
        kernel_blocks = [whole[i] for i in range(n)]
        split = lax.all_to_all(measured, "coil", split_axis=4, concat_axis=2, tiled=True)
        split = jnp.pad(split, [(0, 0)] * 4 + [(0, -width % LANES)])
        coils = measured.shape[2]
        lines_blocks = [split[:, :, i * coils : (i + 1) * coils] for i in range(n)]
        order = ids * jnp.array([0, 1, 1], jnp.int32)
    mine, high, low, lines = summary(order, offsets, kernel_blocks, lines_blocks, taps)
    other = swap(mine, "seg", 1)
    half = compose(ids, mine, other, cols)
    near = [half] + [swap(half, "seg", 2 * i) for i in range(1, chips)]
    far = [swap(part, "seg", 1) for part in near]
    blocks = finish(order, offsets, high, low, lines, mine, other, near, far)
    if order is ids:
        blocks = [blocks[0]] + [swap(blocks[i], "coil", i) for i in range(1, n)]
        return tuple(unpack(blocks, ids))
    states = lax.all_to_all(jnp.stack(blocks), "coil", split_axis=0, concat_axis=0)[..., :width]
    states = jnp.moveaxis(states, 0, 5)
    states = states.reshape(states.shape[:5] + (n * width,))
    return states[0], states[1]


def solution(mesh):
    placed = (
        P("seg", None, "coil", None, None),
        P("seg", None, None, "coil"),
        P("seg", None, None, "coil"),
        P("seg", None, None),
    )
    return jax.shard_map(
        shards,
        mesh=mesh,
        in_specs=placed,
        out_specs=(P("seg", None, "coil", None, None), P("seg", None, "coil", None, None)),
        check_vma=False,
    )
```

```python
import functools

import jax
import jax.numpy as jnp
from jax import lax
from jax.experimental import pallas as pl
from jax.experimental.pallas import tpu as pltpu
from jax.sharding import PartitionSpec as P

F32 = jnp.float32
BF16 = jnp.bfloat16
VMEM = pl.BlockSpec(memory_space=pltpu.VMEM)
SMEM = pl.BlockSpec(memory_space=pltpu.SMEM)
ANY = pl.BlockSpec(memory_space=pl.ANY)
HBM = pl.BlockSpec(memory_space=pltpu.HBM)
LANES = 128
PARAMS = pltpu.CompilerParams(vmem_limit_bytes=40 * 2**20)


def call(body, name, out_shape, in_specs, scratch=(), out_specs=None):
    return pl.pallas_call(
        body,
        out_shape=[jax.ShapeDtypeStruct(shape, dtype) for shape, dtype in out_shape],
        in_specs=in_specs,
        out_specs=out_specs or [VMEM] * len(out_shape),
        scratch_shapes=list(scratch),
        compiler_params=PARAMS,
        name=name,
    )


def halves(a):
    high = a.astype(BF16)
    return high, (a - high.astype(F32)).astype(BF16)


def product(left, right):
    dot = functools.partial(jnp.dot, preferred_element_type=F32)
    high, low = left
    other_high, other_low = halves(right)
    return dot(high, other_high) + (dot(high, other_low) + dot(low, other_high))


def real_form(columns):
    size = columns.shape[0] // 2
    return jnp.concatenate([columns, jnp.concatenate([-columns[size:], columns[:size]], axis=0)], axis=1)


def pick(value, state, picked, offsets, row):
    taps = offsets.shape[1]
    size, lines = picked.shape[1], state.shape[1] * taps // picked.shape[1]
    coils = size // 2 // taps
    chunks = value.shape[1] // LANES
    for i in range(chunks):
        state[i] = value[:, i * LANES : (i + 1) * LANES]
        for part in range(2):
            for tap in range(taps):
                source = pl.ds(part * coils * lines + offsets[row, tap], coils, stride=lines)
                picked[i, pl.ds(part * coils * taps + tap, coils, stride=taps), :] = state[i, source, :]
    return jnp.concatenate([picked[i] for i in range(chunks)], axis=1)


def pick_scratch(lanes, state, size):
    return [pltpu.VMEM((lanes // LANES, state, LANES), F32), pltpu.VMEM((lanes // LANES, size, LANES), F32)]


def visits(segs, backward):
    if backward:
        return [(s, segs + s - 1 if s else 2 * segs + 1) for s in reversed(range(segs))]
    return [(s, s + 1 if s < segs - 1 else 2 * segs) for s in range(segs)]


def through(maps, sources, choose, backward):
    state = None
    for s, row in visits(len(sources), backward):
        state = sources[s] if state is None else product(maps(s), carried) + sources[s]
        carried = choose(state, row=row)
    return carried


def spot(ids, i):
    return lax.bitwise_xor(ids[0], i)


def pack(measured, ids):
    segs, parts, coils, lines, samples = measured.shape
    n = lax.axis_size("coil")
    width = samples // n

    def body(ids_ref, m_ref, *rest):
        outs, sems = rest[:n], rest[n]
        copies = []
        for i in range(n):
            start = pl.multiple_of(spot(ids_ref, i) * width, width)
            copies.append(pltpu.make_async_copy(m_ref.at[:, :, :, :, pl.ds(start, width)], outs[i], sems.at[i]))
        for c in copies:
            c.start()
        for c in copies:
            c.wait()

    out = ((segs, parts, coils, lines, width), F32)
    return call(body, "pack", [out] * n, [SMEM, HBM], [pltpu.SemaphoreType.DMA((n,))])(ids, measured)


def hold(first, kernels, offsets):
    def body(_, k_ref, o_ref, k_out, f_out, b_out):
        k_out[...] = k_ref[...]
        f_out[...] = o_ref[:1, 0]
        b_out[...] = o_ref[-1:, 1]

    edge = ((1, offsets.shape[2]), jnp.int32)
    return call(body, "hold", [(kernels.shape, F32), edge, edge], [ANY, VMEM, VMEM])(first, kernels, offsets)


def gather(ids, blocks):
    n = len(blocks)
    segs, parts, coils, lines, width = blocks[0].shape

    def body(ids_ref, *refs):
        for i in range(n):
            refs[n][:, :, pl.ds(spot(ids_ref, i) * coils, coils)] = refs[i][...]

    out = ((segs, parts, n * coils, lines, width), F32)
    return call(body, "gather", [out], [SMEM] + [VMEM] * n)(ids, *blocks)[0]


def prepare(ids, offsets, blocks, backward):
    n = len(blocks)
    segs, _, block_cols, rows = blocks[0].shape
    cols = block_cols * n
    size = 2 * cols

    def body(ids_ref, off_ref, *refs):
        hi_ref, lo_ref, c_ref, kt, state, picked = refs[n:]
        choose = functools.partial(pick, state=state, picked=picked, offsets=off_ref)
        for i in range(n):
            kt[:, :, pl.ds(spot(ids_ref, i), 1)] = refs[i][...][:, :, None]
        columns = []
        for s in range(segs):
            real, imag = (kt[s, part].reshape(cols, rows).T for part in range(2))
            columns.append(jnp.concatenate([real, imag], axis=0))
            hi_ref[s], lo_ref[s] = halves(real_form(columns[s]))
        first = visits(segs, backward)[0][0]
        sources = [columns[s] if s == first else jnp.zeros_like(columns[s]) for s in range(segs)]
        c_ref[...] = through(lambda s: (hi_ref[s], lo_ref[s]), sources, choose, backward)

    return call(
        body,
        "prepare_backward" if backward else "prepare_forward",
        [((segs, 2 * rows, size), BF16)] * 2 + [((size, cols), F32)],
        [SMEM, SMEM] + [VMEM] * n,
        [pltpu.VMEM((segs, 2, n, block_cols, rows), F32)] + pick_scratch(cols, 2 * rows, size),
    )(ids, offsets, *blocks)


def summary(offsets, maps, measured):
    high, low, columns = maps
    size, cols = columns.shape
    segs, parts, coils, lines, width = measured.shape
    rows = parts * coils * lines

    def body(off_ref, hi_ref, lo_ref, c_ref, m_ref, e_ref, state, picked):
        choose = functools.partial(pick, state=state, picked=picked, offsets=off_ref)
        e_ref[:, :cols] = c_ref[...]
        sources = [m_ref[s].reshape(rows, width) for s in range(segs)]
        e_ref[:, cols:] = through(lambda s: (hi_ref[s], lo_ref[s]), sources, choose, False)
    return call(
        body,
        "summary",
        [((size, cols + width), F32)],
        [SMEM] + [VMEM] * 4,
        pick_scratch(width, rows, size),
    )(offsets, high, low, columns, measured)[0]


def compose(ids, mine, other, cols, backward):
    size, lanes = mine.shape

    def body(ids_ref, a_ref, b_ref, out_ref, pair, whole):
        core = ids_ref[2]
        pair[pl.ds(core, 1)] = a_ref[...][None]
        pair[pl.ds(1 - core, 1)] = b_ref[...][None]
        near, far = (pair[1], pair[0]) if backward else (pair[0], pair[1])
        both = product(halves(real_form(far[:, :cols])), near)
        whole[:, :cols] = both[:, :cols]
        whole[:, cols:] = both[:, cols:] + far[:, cols:]
        out_ref[...] = whole[pl.ds(pl.multiple_of(core * (size // 2), size // 2), size // 2), :]

    return call(
        body,
        "compose_backward" if backward else "compose_forward",
        [((size // 2, lanes), F32)],
        [SMEM, VMEM, VMEM],
        [pltpu.VMEM((2, size, lanes), F32), pltpu.VMEM((size, lanes), F32)],
    )(ids, mine, other)[0]


def finish(ids, offsets, maps, sources, mine, other, near, far, backward, following=None, arrived=()):
    high, low, _ = maps
    segs, _, coils, lines, width = sources.shape
    _, rows, size = high.shape
    cols = size // 2
    lanes = mine.shape[1]
    chips = len(near)
    n = lax.axis_size("coil")
    own_coils = coils // n
    extra = list(following) if following else []
    homes = len(arrived)

    def body(ids_ref, off_ref, hi_ref, lo_ref, m_ref, a_ref, b_ref, *refs):
        near_refs, far_refs, refs = refs[:chips], refs[chips : 2 * chips], refs[2 * chips :]
        home_refs, refs = refs[:homes], refs[homes:]
        extra_refs, outs, refs = refs[: len(extra)], refs[len(extra) : len(extra) + n + 1], refs[len(extra) + n + 1 :]
        if extra:
            e_ref, refs = refs[0], refs[1:]
        if homes:
            home_out, refs = refs[0], refs[1:]
        pair, table, carried, state, picked = refs[:5]
        copies = unpack_copies(ids_ref, home_refs, home_out, refs[5]) if homes else []
        for c in copies:
            c.start()
        choose = functools.partial(pick, state=state, picked=picked, offsets=off_ref)
        chip, core = ids_ref[1], ids_ref[2]
        pair[pl.ds(core, 1)] = a_ref[...][None]
        pair[pl.ds(1 - core, 1)] = b_ref[...][None]
        for i in range(chips):
            e = lax.bitwise_xor(chip, i)
            table[pl.ds(e * 2 + core, 1)] = near_refs[i][...][None]
            table[pl.ds(e * 2 + 1 - core, 1)] = far_refs[i][...][None]

        def step(block, value):
            return product(halves(real_form(block[:, :cols])), value) + block[:, cols:]

        order = list(range(chips))[:: -1 if backward else 1]
        value = jnp.zeros((size, width), F32)
        carried[order[0]] = value
        for at, e in enumerate(order[:-1]):
            block = jnp.concatenate([table[2 * e], table[2 * e + 1]], axis=0)
            value = step(block, value) if at else block[:, cols:]
            carried[order[at + 1]] = value
        value = carried[chip]
        leading = 1 if backward else 0
        value = jnp.where(core == leading, value, step(pair[leading], value))
        states = [None] * segs
        for at, (s, row) in enumerate(visits(segs, backward)):
            states[s] = product((hi_ref[s], lo_ref[s]), value) + m_ref[s].reshape(rows, width)
            if at < segs - 1:
                value = choose(states[s], row=row)
        for s in range(segs):
            outs[n][s] = states[s].reshape(2, coils, lines, width)
        for i in range(n):
            outs[i][...] = outs[n][:, :, pl.ds(spot(ids_ref, i) * own_coils, own_coils)]
        if extra:
            next_hi, next_lo, next_columns = extra_refs
            e_ref[:, :cols] = next_columns[...]
            e_ref[:, cols:] = through(lambda s: (next_hi[s], next_lo[s]), states, choose, not backward)
        for c in copies:
            c.wait()

    out_shape = [((segs, 2, own_coils, lines, width), F32)] * n + [((segs, 2, coils, lines, width), F32)]
    if extra:
        out_shape.append(((size, lanes), F32))
    out_specs = [VMEM] * len(out_shape)
    if homes:
        out_shape.append(((segs, 2, own_coils, lines, n * width), F32))
        out_specs.append(ANY)
    return call(
        body,
        "finish_backward" if backward else "finish_forward",
        out_shape,
        [SMEM, SMEM] + [VMEM] * (5 + 2 * chips + homes + len(extra)),
        [
            pltpu.VMEM((2, size, lanes), F32),
            pltpu.VMEM((2 * chips, size // 2, lanes), F32),
            pltpu.VMEM((chips, size, width), F32),
        ]
        + pick_scratch(width, rows, size)
        + [pltpu.SemaphoreType.DMA((n,))] * bool(homes),
        out_specs,
    )(ids, offsets, high, low, sources, mine, other, *near, *far, *arrived, *extra)


def unpack_copies(ids, ins, out, sems):
    width = ins[0].shape[-1]
    copies = []
    for i, block in enumerate(ins):
        start = pl.multiple_of(spot(ids, i) * width, width)
        copies.append(pltpu.make_async_copy(block, out.at[:, :, :, :, pl.ds(start, width)], sems.at[i]))
    return copies


def unpack(blocks, ids):
    n = len(blocks)
    segs, parts, coils, lines, width = blocks[0].shape

    def body(ids_ref, *refs):
        copies = unpack_copies(ids_ref, refs[:n], refs[n], refs[n + 1])
        for c in copies:
            c.start()
        for c in copies:
            c.wait()

    return call(
        body,
        "unpack",
        [((segs, parts, coils, lines, n * width), F32)],
        [SMEM] + [VMEM] * n,
        [pltpu.SemaphoreType.DMA((n,))],
        [ANY],
    )(ids, *blocks)[0]


def swap(block, axis, distance):
    return lax.ppermute(block, axis, [(i, i ^ distance) for i in range(lax.axis_size(axis))])


def spread_kernels(own):
    n = lax.axis_size("coil")
    blocks = {0: own}
    distance = n // 2
    while distance:
        for i in sorted(blocks):
            blocks[i ^ distance] = swap(blocks[i], "coil", distance)
        distance //= 2
    return [blocks[i] for i in range(n)]


def spread_summary(ids, mine, cols, backward):
    chips = lax.axis_size("seg") // 2
    other = swap(mine, "seg", 1)
    half = compose(ids, mine, other, cols, backward)
    near = [half] + [swap(half, "seg", 2 * i) for i in range(1, chips)]
    far = [swap(part, "seg", 1) for part in near]
    return mine, other, near, far


def shards(measured, forward_kernel, backward_kernel, line_offsets):
    n = lax.axis_size("coil")
    places = lax.axis_size("seg")
    coil, seg = lax.axis_index("coil"), lax.axis_index("seg")
    taps = line_offsets.shape[2]
    width = measured.shape[4] // n
    cols = forward_kernel.shape[3] * n
    ids = jnp.stack([coil, seg // 2, seg % 2]).astype(jnp.int32)
    kernels_f, kernels_b = (jnp.swapaxes(k, 2, 3) for k in (forward_kernel, backward_kernel))
    aligned = width % LANES == 0 and (cols // taps // n) % 8 == 0
    if aligned:
        order = ids
        forward_blocks = spread_kernels(kernels_f)
        pieces = pack(measured, ids)
        lines_blocks = [pieces[0]] + [swap(pieces[i], "coil", i) for i in range(1, n)]
    else:
        order = ids * jnp.array([0, 1, 1], jnp.int32)
        forward_blocks = list(lax.all_gather(kernels_f, "coil"))
        split = lax.all_to_all(measured, "coil", split_axis=4, concat_axis=2, tiled=True)
        split = jnp.pad(split, [(0, 0)] * 4 + [(0, -width % LANES)])
        lines_blocks = jnp.split(split, n, axis=2)
    kernels_b, first, last = hold(lines_blocks[1], kernels_b, line_offsets)
    after = lax.ppermute(first, "seg", [(i + 1, i) for i in range(places - 1)])
    before = lax.ppermute(last, "seg", [(i, i + 1) for i in range(places - 1)])
    offsets = jnp.concatenate([line_offsets[:, 0], line_offsets[:, 1], after, before])
    lines = gather(order, lines_blocks)
    forward_maps = prepare(order, offsets, forward_blocks, False)
    mine = summary(offsets, forward_maps, lines)
    backward_blocks = spread_kernels(kernels_b) if aligned else list(lax.all_gather(kernels_b, "coil"))
    backward_maps = prepare(order, offsets, backward_blocks, True)
    shared = spread_summary(ids, mine, cols, False)
    *forward_out, forward, mine = finish(order, offsets, forward_maps, lines, *shared, False, backward_maps)
    shared = spread_summary(ids, mine, cols, True)

    def home(blocks):
        return [blocks[0]] + [swap(blocks[i], "coil", i) for i in range(1, n)]

    if aligned:
        *result_out, _, forward = finish(order, offsets, backward_maps, forward, *shared, True, arrived=home(forward_out))
        return forward, unpack(home(result_out), ids)
    *result_out, _ = finish(order, offsets, backward_maps, forward, *shared, True)

    def rejoin(blocks):
        states = lax.all_to_all(jnp.stack(blocks), "coil", split_axis=0, concat_axis=0)[..., :width]
        states = jnp.moveaxis(states, 0, 4)
        return states.reshape(states.shape[:4] + (n * width,))

    return rejoin(forward_out), rejoin(result_out)


def solution(mesh):
    placed = (
        P("seg", None, "coil", None, None),
        P("seg", None, None, "coil"),
        P("seg", None, None, "coil"),
        P("seg", None, None),
    )
    return jax.shard_map(
        shards,
        mesh=mesh,
        in_specs=placed,
        out_specs=(P("seg", None, "coil", None, None), P("seg", None, "coil", None, None)),
        check_vma=False,
    )
```

```python
import functools

import jax
import jax.numpy as jnp
from jax import lax
from jax.experimental import pallas as pl
from jax.experimental.pallas import tpu as pltpu
from jax.sharding import PartitionSpec as P

F32 = jnp.float32
BF16 = jnp.bfloat16
VMEM = pl.BlockSpec(memory_space=pltpu.VMEM)
ANY = pl.BlockSpec(memory_space=pl.ANY)
HBM = pl.BlockSpec(memory_space=pltpu.HBM)
LANES = 128
PARAMS = pltpu.CompilerParams(vmem_limit_bytes=40 * 2**20)


def call(body, name, out_shape, in_specs, scratch=(), out_specs=None, after=()):
    def whole(*refs):
        body(*refs[len(after) :])

    kernel = pl.pallas_call(
        whole,
        out_shape=[jax.ShapeDtypeStruct(shape, dtype) for shape, dtype in out_shape],
        in_specs=[ANY] * len(after) + in_specs,
        out_specs=out_specs or [VMEM] * len(out_shape),
        scratch_shapes=list(scratch),
        compiler_params=PARAMS,
        name=name,
    )
    return functools.partial(kernel, *after)


def halves(a):
    high = a.astype(BF16)
    return high, (a - high.astype(F32)).astype(BF16)


def product(left, right):
    dot = functools.partial(jnp.dot, preferred_element_type=F32)
    high, low = left
    other_high, other_low = halves(right)
    width = right.shape[1]
    if width > LANES:
        return dot(high, other_high) + (dot(high, other_low) + dot(low, other_high))
    both = dot(high, jnp.concatenate([other_high, other_low], axis=1))
    return both[:, :width] + (both[:, width:] + dot(low, other_high))


def real_form(columns):
    size = columns.shape[0] // 2
    return jnp.concatenate([columns, jnp.concatenate([-columns[size:], columns[:size]], axis=0)], axis=1)


def pick(value, state, picked, offsets, coils, row):
    taps, lines = picked.shape[1] // 2 // coils, state.shape[1] // 2 // coils
    chunks = value.shape[1] // LANES
    for i in range(chunks):
        state[i] = value[:, i * LANES : (i + 1) * LANES]
        for part in range(2):
            for tap in range(taps):
                source = pl.ds(part * coils * lines + offsets[row, tap], coils, stride=lines)
                picked[i, pl.ds(part * coils * taps + tap, coils, stride=taps), :] = state[i, source, :]
    return jnp.concatenate([picked[i] for i in range(chunks)], axis=1)


def pick_scratch(lanes, state, size):
    return [pltpu.VMEM((lanes // LANES, state, LANES), F32), pltpu.VMEM((lanes // LANES, size, LANES), F32)]


def offset_scratch(offsets):
    return [pltpu.SMEM(offsets.shape, jnp.int32), pltpu.SemaphoreType.DMA]


def visits(segs, backward):
    if backward:
        return [(s, segs + s - 1 if s else 2 * segs + 1) for s in reversed(range(segs))]
    return [(s, s + 1 if s < segs - 1 else 2 * segs) for s in range(segs)]


def walk(maps, carried, sources, choose, backward):
    states = list(sources)
    for s, row in visits(len(sources), backward):
        if carried is not None:
            states[s] = product(maps(s), carried) + sources[s]
        carried = choose(states[s], row=row)
    return states, carried


def response(high, low, states, choose, backward):
    size = high.shape[2]
    first = visits(len(states), backward)[0][0]
    columns = high[first, :, : size // 2].astype(F32) + low[first, :, : size // 2].astype(F32)
    blank = jnp.zeros_like(columns)
    sources = [jnp.concatenate([columns if s == first else blank, state], axis=1) for s, state in enumerate(states)]
    return walk(lambda s: (high[s], low[s]), None, sources, choose, backward)[1]


def spot(near, i):
    return lax.bitwise_xor(lax.axis_index("coil"), i) if near else i


def my_chip():
    seg = lax.axis_index("seg")
    return lax.shift_right_logical(seg, 1), lax.bitwise_and(seg, 1)


def pack(measured):
    segs, parts, coils, lines, samples = measured.shape
    n = lax.axis_size("coil")
    width = samples // n

    def body(m_ref, *rest):
        outs, sems = rest[:n], rest[n]
        copies = []
        for i in range(n):
            start = pl.multiple_of(spot(True, i) * width, width)
            copies.append(pltpu.make_async_copy(m_ref.at[:, :, :, :, pl.ds(start, width)], outs[i], sems.at[i]))
        for c in copies:
            c.start()
        for c in copies:
            c.wait()

    out = ((segs, parts, coils, lines, width), F32)
    return call(body, "pack", [out] * n, [HBM], [pltpu.SemaphoreType.DMA((n,))])(measured)


def hold(first, *values):
    def body(_, *refs):
        for i in range(len(values)):
            refs[len(values) + i][...] = refs[i][...]

    out_shape = [(v.shape, v.dtype) for v in values]
    return call(body, "hold", out_shape, [ANY] + [VMEM] * len(values))(first, *values)


def gather(near, blocks, after):
    n = len(blocks)
    segs, parts, coils, lines, width = blocks[0].shape

    def body(*refs):
        for i in range(n):
            refs[n][:, :, pl.ds(spot(near, i) * coils, coils)] = refs[i][...]

    out = ((segs, parts, n * coils, lines, width), F32)
    return call(body, "gather", [out], [VMEM] * n, after=after)(*blocks)[0]


def prepare(near, blocks, backward):
    n = len(blocks)
    segs, _, block_cols, rows = blocks[0].shape
    cols = block_cols * n
    size = 2 * cols

    def body(*refs):
        hi_ref, lo_ref, kt = refs[n:]
        for i in range(n):
            kt[:, :, pl.ds(spot(near, i), 1)] = refs[i][...][:, :, None]
        for s in range(segs):
            real, imag = (kt[s, part].reshape(cols, rows).T for part in range(2))
            hi_ref[s], lo_ref[s] = halves(real_form(jnp.concatenate([real, imag], axis=0)))

    return call(
        body,
        "prepare_backward" if backward else "prepare_forward",
        [((segs, 2 * rows, size), BF16)] * 2,
        [VMEM] * n,
        [pltpu.VMEM((segs, 2, n, block_cols, rows), F32)],
    )(*blocks)


def summary(offsets, maps, measured):
    high, low = maps
    _, rows, size = high.shape
    segs, _, coils, _, width = measured.shape
    lanes = size // 2 + width

    def body(off_ref, hi_ref, lo_ref, m_ref, e_ref, state, picked, off, sem):
        fetch = pltpu.make_async_copy(off_ref, off, sem)
        fetch.start()
        fetch.wait()
        choose = functools.partial(pick, state=state, picked=picked, offsets=off, coils=coils)
        e_ref[...] = response(hi_ref, lo_ref, [m_ref[s].reshape(rows, width) for s in range(segs)], choose, False)

    return call(
        body,
        "summary",
        [((size, lanes), F32)],
        [VMEM] * 4,
        pick_scratch(lanes, rows, size) + offset_scratch(offsets),
    )(offsets, high, low, measured)[0]


def compose(mine, other, cols, backward):
    size, lanes = mine.shape

    def body(a_ref, b_ref, whole, out_ref, pair):
        _, core = my_chip()
        pair[pl.ds(core, 1)] = a_ref[...][None]
        pair[pl.ds(1 - core, 1)] = b_ref[...][None]
        near, far = (pair[1], pair[0]) if backward else (pair[0], pair[1])
        both = product(halves(real_form(far[:, :cols])), near)
        whole[:, :cols] = both[:, :cols]
        whole[:, cols:] = both[:, cols:] + far[:, cols:]
        out_ref[...] = whole[pl.ds(pl.multiple_of(core * (size // 2), size // 2), size // 2), :]

    return call(
        body,
        "compose_backward" if backward else "compose_forward",
        [((size, lanes), F32), ((size // 2, lanes), F32)],
        [VMEM, VMEM],
        [pltpu.VMEM((2, size, lanes), F32)],
    )(mine, other)


def incoming(own, parts, table, carried, backward):
    chips, _, cols, _ = table.shape
    chip, core = my_chip()
    table[pl.ds(chip, 1)] = own[...].reshape((1,) + table.shape[1:])
    for i in range(1, chips):
        e = lax.bitwise_xor(chip, i)
        table[pl.ds(e, 1), pl.ds(core, 1)] = parts[2 * i - 2][...][None, None]
        table[pl.ds(e, 1), pl.ds(1 - core, 1)] = parts[2 * i - 1][...][None, None]
    order = list(range(chips))[:: -1 if backward else 1]
    carried[order[0]] = jnp.zeros(carried.shape[1:], F32)
    value = None
    for at, e in enumerate(order[:-1]):
        block = table[e].reshape(2 * cols, -1)
        if value is None:
            value = block[:, cols:]
        else:
            value = product(halves(real_form(block[:, :cols])), value) + block[:, cols:]
        carried[order[at + 1]] = value
    return carried[chip]


def incoming_scratch(chips, size, lanes):
    return [pltpu.VMEM((chips, 2, size // 2, lanes), F32), pltpu.VMEM((chips, size, lanes - size // 2), F32)]


def finish(near, offsets, maps, sources, mine, other, blocks, backward, following=(), joined=None, after=()):
    high, low = maps
    segs, _, coils, lines, width = sources.shape
    _, rows, size = high.shape
    cols, lanes = size // 2, mine.shape[1]
    chips = (len(blocks) + 1) // 2
    n = lax.axis_size("coil")
    own_coils = coils // n
    extra = list(following) + ([] if joined is None else [joined])

    def body(off_ref, hi_ref, lo_ref, m_ref, a_ref, b_ref, own, *refs):
        at = 2 * chips - 2
        rest, extra_refs, refs = refs[:at], refs[at : at + len(extra)], refs[at + len(extra) :]
        outs, refs = refs[:n], refs[n:]
        if following:
            e_ref, refs = refs[0], refs[1:]
        whole, table, carried, state, picked, off, sem = refs
        fetch = pltpu.make_async_copy(off_ref, off, sem)
        fetch.start()
        choose = functools.partial(pick, state=state, picked=picked, offsets=off, coils=coils)
        value = incoming(own, rest, table, carried, backward)
        moved = product(halves(real_form(b_ref[:, :cols])), value) + b_ref[:, cols:]
        value = jnp.where(my_chip()[1] == (1 if backward else 0), value, moved)
        fetch.wait()
        source = [m_ref[s].reshape(rows, width) for s in range(segs)]
        states, _ = walk(lambda s: (hi_ref[s], lo_ref[s]), value, source, choose, backward)
        if following:
            e_ref[...] = response(extra_refs[0], extra_refs[1], states, choose, not backward)
        for s in range(segs):
            whole[s] = states[s].reshape(2, coils, lines, width)
        for i in range(n):
            cut = whole[:, :, pl.ds(spot(near, i) * own_coils, own_coils)]
            if joined is not None and i == 1:
                outs[i][0] = extra_refs[-1][...]
                outs[i][1] = cut
            else:
                outs[i][...] = cut

    block = (segs, 2, own_coils, lines, width)
    out_shape = [((2, *block) if joined is not None and i == 1 else block, F32) for i in range(n)]
    scratch = [pltpu.VMEM(sources.shape, F32)]
    if following:
        out_shape += [((size, lanes), F32), (sources.shape, F32)]
        scratch = []
    return call(
        body,
        "finish_backward" if backward else "finish_forward",
        out_shape,
        [VMEM] * (6 + len(blocks) + len(extra)),
        scratch
        + incoming_scratch(chips, size, lanes)
        + pick_scratch(lanes if following else width, rows, size)
        + offset_scratch(offsets),
        after=after,
    )(offsets, high, low, sources, mine, other, *blocks, *extra)


def unpack(forward, result, joined):
    n = len(forward)
    segs, parts, coils, lines, width = forward[0].shape
    sent = [forward[0], result[0], joined] + [b for i in range(2, n) for b in (forward[i], result[i])]

    def body(*refs):
        ins, outs, sems = refs[: len(sent)], refs[len(sent) : len(sent) + 2], refs[len(sent) + 2]
        copies = []
        for i in range(n):
            start = pl.multiple_of(spot(True, i) * width, width)
            for o in range(2):
                source = ins[2].at[o] if i == 1 else ins[o if i == 0 else 2 * i - 1 + o]
                copies.append(pltpu.make_async_copy(source, outs[o].at[:, :, :, :, pl.ds(start, width)], sems.at[i, o]))
        for c in copies:
            c.start()
        for c in copies:
            c.wait()

    return call(
        body,
        "unpack",
        [((segs, parts, coils, lines, n * width), F32)] * 2,
        [VMEM] * len(sent),
        [pltpu.SemaphoreType.DMA((n, 2))],
        [ANY] * 2,
    )(*sent)


def swap(block, axis, distance):
    return lax.ppermute(block, axis, [(i, i ^ distance) for i in range(lax.axis_size(axis))])


def spread_kernels(own):
    n = lax.axis_size("coil")
    blocks = {0: own}
    distance = n // 2
    while distance:
        blocks.update({i ^ distance: swap(blocks[i], "coil", distance) for i in sorted(blocks)})
        distance //= 2
    return [blocks[i] for i in range(n)]


def exchange(whole, half, first=None):
    chips = lax.axis_size("seg") // 2
    blocks = [whole]
    for i in range(1, chips):
        block = swap(half, "seg", 2 * i)
        if i == min(2, chips - 1) and first is not None:
            (block,) = hold(first, block)
        blocks += [block, swap(block, "seg", 1)]
    return blocks


def shards(measured, forward_kernel, backward_kernel, line_offsets):
    n = lax.axis_size("coil")
    places = lax.axis_size("seg")
    taps = line_offsets.shape[2]
    width = measured.shape[4] // n
    cols = forward_kernel.shape[3] * n
    first, last = line_offsets[0, 0], line_offsets[-1, 1]
    kernels_f, kernels_b = (jnp.swapaxes(k, 2, 3) for k in (forward_kernel, backward_kernel))
    aligned = width % LANES == 0 and (cols // taps // n) % 8 == 0
    if aligned:
        forward_blocks = spread_kernels(kernels_f)
        backward_blocks = spread_kernels(kernels_b)
        pieces = pack(measured)
        lines_blocks = [pieces[0]] + [swap(pieces[i], "coil", i) for i in range(1, n)]
        first, last = hold(forward_blocks[1], first, last)
    else:
        forward_blocks = list(lax.all_gather(kernels_f, "coil"))
        backward_blocks = list(lax.all_gather(kernels_b, "coil"))
        split = lax.all_to_all(measured, "coil", split_axis=4, concat_axis=2, tiled=True)
        split = jnp.pad(split, [(0, 0)] * 4 + [(0, -width % LANES)])
        lines_blocks = jnp.split(split, n, axis=2)
    after = lax.ppermute(first, "seg", [(i + 1, i) for i in range(places - 1)])[None]
    before = lax.ppermute(last, "seg", [(i, i + 1) for i in range(places - 1)])[None]
    offsets = jnp.concatenate([line_offsets[:, 0], line_offsets[:, 1], after, before])
    offsets = jnp.pad(offsets, [(0, -offsets.shape[0] % 8), (0, LANES - taps)])

    forward_maps = prepare(aligned, forward_blocks, False)
    lines = gather(aligned, lines_blocks, forward_maps[:1])
    backward_maps = prepare(aligned, backward_blocks, True)
    mine = summary(offsets, forward_maps, lines)
    other = swap(mine, "seg", 1)
    blocks = exchange(*compose(mine, other, cols, False))
    *forward_out, mine, forward = finish(aligned, offsets, forward_maps, lines, mine, other, blocks, False, backward_maps)
    other = swap(mine, "seg", 1)
    whole, half = compose(mine, other, cols, True)
    if aligned:
        home = dict(enumerate(forward_out[:2])) | {i: swap(forward_out[i], "coil", i) for i in range(2, n)}
        blocks = exchange(whole, half, home[n - 1] if n > 2 else None)
        result_out = finish(
            aligned,
            offsets,
            backward_maps,
            forward,
            mine,
            other,
            blocks,
            True,
            joined=forward_out[1],
            after=[home[i] for i in range(2, n - 1)],
        )
        result_home = [result_out[0]] + [swap(result_out[i], "coil", i) for i in range(1, n)]
        return tuple(unpack(home, result_home, result_home[1]))
    blocks = exchange(whole, half)
    result_out = finish(aligned, offsets, backward_maps, forward, mine, other, blocks, True)

    def rejoin(blocks):
        states = lax.all_to_all(jnp.stack(blocks), "coil", split_axis=0, concat_axis=0)[..., :width]
        states = jnp.moveaxis(states, 0, 4)
        return states.reshape(states.shape[:4] + (n * width,))

    return rejoin(forward_out), rejoin(result_out)


def solution(mesh):
    placed = (
        P("seg", None, "coil", None, None),
        P("seg", None, None, "coil"),
        P("seg", None, None, "coil"),
        P("seg", None, None),
    )
    return jax.shard_map(
        shards,
        mesh=mesh,
        in_specs=placed,
        out_specs=(P("seg", None, "coil", None, None), P("seg", None, "coil", None, None)),
        check_vma=False,
    )
```

```python
import functools

import jax
import jax.numpy as jnp
from jax import lax
from jax.experimental import pallas as pl
from jax.experimental.pallas import tpu as pltpu
from jax.sharding import PartitionSpec as P

F32 = jnp.float32
BF16 = jnp.bfloat16
VMEM = pl.BlockSpec(memory_space=pltpu.VMEM)
ANY = pl.BlockSpec(memory_space=pl.ANY)
HBM = pl.BlockSpec(memory_space=pltpu.HBM)
LANES = 128
PARAMS = pltpu.CompilerParams(vmem_limit_bytes=40 * 2**20)


def call(body, name, out_shape, in_specs, scratch=(), out_specs=None, after=()):
    def whole(*refs):
        body(*refs[len(after) :])

    kernel = pl.pallas_call(
        whole,
        out_shape=[jax.ShapeDtypeStruct(shape, dtype) for shape, dtype in out_shape],
        in_specs=[ANY] * len(after) + in_specs,
        out_specs=out_specs or [VMEM] * len(out_shape),
        scratch_shapes=list(scratch),
        compiler_params=PARAMS,
        name=name,
    )
    return functools.partial(kernel, *after)


def halves(a):
    high = a.astype(BF16)
    return high, (a - high.astype(F32)).astype(BF16)


def product(left, right):
    dot = functools.partial(jnp.dot, preferred_element_type=F32)
    high, low = left
    other_high, other_low = halves(right)
    width = right.shape[1]
    if width > LANES:
        return dot(high, other_high) + (dot(high, other_low) + dot(low, other_high))
    both = dot(high, jnp.concatenate([other_high, other_low], axis=1))
    return both[:, :width] + (both[:, width:] + dot(low, other_high))


def real_form(columns):
    size = columns.shape[0] // 2
    return jnp.concatenate([columns, jnp.concatenate([-columns[size:], columns[:size]], axis=0)], axis=1)


def pick(value, state, picked, offsets, coils, row):
    taps, lines = picked.shape[1] // 2 // coils, state.shape[1] // 2 // coils
    line = [jnp.sum(offsets[row : row + 1, tap : tap + 1]) for tap in range(taps)]
    chunks = value.shape[1] // LANES
    for i in range(chunks):
        state[i] = value[:, i * LANES : (i + 1) * LANES]
        for part in range(2):
            for tap in range(taps):
                source = pl.ds(part * coils * lines + line[tap], coils, stride=lines)
                picked[i, pl.ds(part * coils * taps + tap, coils, stride=taps), :] = state[i, source, :]
    return jnp.concatenate([picked[i] for i in range(chunks)], axis=1)


def pick_scratch(lanes, state, size):
    return [pltpu.VMEM((lanes // LANES, state, LANES), F32), pltpu.VMEM((lanes // LANES, size, LANES), F32)]


def visits(segs, backward):
    if backward:
        return [(s, segs + s - 1 if s else 2 * segs + 1) for s in reversed(range(segs))]
    return [(s, s + 1 if s < segs - 1 else 2 * segs) for s in range(segs)]


def walk(maps, carried, sources, choose, backward):
    states = list(sources)
    for s, row in visits(len(sources), backward):
        if carried is not None:
            states[s] = product(maps(s), carried) + sources[s]
        carried = choose(states[s], row=row)
    return states, carried


def response(high, low, states, choose, backward):
    size = high.shape[2]
    first = visits(len(states), backward)[0][0]
    columns = high[first, :, : size // 2].astype(F32) + low[first, :, : size // 2].astype(F32)
    blank = jnp.zeros_like(columns)
    sources = [jnp.concatenate([columns if s == first else blank, state], axis=1) for s, state in enumerate(states)]
    return walk(lambda s: (high[s], low[s]), None, sources, choose, backward)[1]


def spot(near, i):
    return lax.bitwise_xor(lax.axis_index("coil"), i) if near else i


def my_chip():
    seg = lax.axis_index("seg")
    return lax.shift_right_logical(seg, 1), lax.bitwise_and(seg, 1)


def pack(measured):
    segs, parts, coils, lines, samples = measured.shape
    n = lax.axis_size("coil")
    width = samples // n

    def body(m_ref, *rest):
        outs, sems = rest[:n], rest[n]
        copies = []
        for i in range(n):
            start = pl.multiple_of(spot(True, i) * width, width)
            copies.append(pltpu.make_async_copy(m_ref.at[:, :, :, :, pl.ds(start, width)], outs[i], sems.at[i]))
        for c in copies:
            c.start()
        for c in copies:
            c.wait()

    out = ((segs, parts, coils, lines, width), F32)
    return call(body, "pack", [out] * n, [HBM], [pltpu.SemaphoreType.DMA((n,))])(measured)


def hold(first, *values):
    def body(_, *refs):
        for i in range(len(values)):
            refs[len(values) + i][...] = refs[i][...]

    out_shape = [(v.shape, v.dtype) for v in values]
    return call(body, "hold", out_shape, [ANY] + [VMEM] * len(values))(first, *values)


def gather(near, blocks, after):
    n = len(blocks)
    segs, parts, coils, lines, width = blocks[0].shape

    def body(*refs):
        for i in range(n):
            refs[n][:, :, pl.ds(spot(near, i) * coils, coils)] = refs[i][...]

    out = ((segs, parts, n * coils, lines, width), F32)
    return call(body, "gather", [out], [VMEM] * n, after=after)(*blocks)[0]


def prepare(near, blocks, backward):
    n = len(blocks)
    segs, _, block_cols, rows = blocks[0].shape
    cols = block_cols * n
    size = 2 * cols

    def body(*refs):
        hi_ref, lo_ref, kt = refs[n:]
        for i in range(n):
            kt[:, :, pl.ds(spot(near, i), 1)] = refs[i][...][:, :, None]
        for s in range(segs):
            real, imag = (kt[s, part].reshape(cols, rows).T for part in range(2))
            hi_ref[s], lo_ref[s] = halves(real_form(jnp.concatenate([real, imag], axis=0)))

    return call(
        body,
        "prepare_backward" if backward else "prepare_forward",
        [((segs, 2 * rows, size), BF16)] * 2,
        [VMEM] * n,
        [pltpu.VMEM((segs, 2, n, block_cols, rows), F32)],
    )(*blocks)


def summary(offsets, maps, measured):
    high, low = maps
    _, rows, size = high.shape
    segs, _, coils, _, width = measured.shape
    lanes = size // 2 + width

    def body(off_ref, hi_ref, lo_ref, m_ref, e_ref, state, picked):
        choose = functools.partial(pick, state=state, picked=picked, offsets=off_ref, coils=coils)
        e_ref[...] = response(hi_ref, lo_ref, [m_ref[s].reshape(rows, width) for s in range(segs)], choose, False)

    return call(
        body,
        "summary",
        [((size, lanes), F32)],
        [VMEM] * 4,
        pick_scratch(lanes, rows, size),
    )(offsets, high, low, measured)[0]


def compose(mine, other, cols, backward):
    size, lanes = mine.shape

    def body(a_ref, b_ref, whole, out_ref, pair):
        _, core = my_chip()
        pair[pl.ds(core, 1)] = a_ref[...][None]
        pair[pl.ds(1 - core, 1)] = b_ref[...][None]
        near, far = (pair[1], pair[0]) if backward else (pair[0], pair[1])
        both = product(halves(real_form(far[:, :cols])), near)
        whole[:, :cols] = both[:, :cols]
        whole[:, cols:] = both[:, cols:] + far[:, cols:]
        out_ref[...] = whole[pl.ds(pl.multiple_of(core * (size // 2), size // 2), size // 2), :]

    return call(
        body,
        "compose_backward" if backward else "compose_forward",
        [((size, lanes), F32), ((size // 2, lanes), F32)],
        [VMEM, VMEM],
        [pltpu.VMEM((2, size, lanes), F32)],
    )(mine, other)


def incoming(own, parts, table, carried, backward):
    chips, _, cols, _ = table.shape
    chip, core = my_chip()
    table[pl.ds(chip, 1)] = own[...].reshape((1,) + table.shape[1:])
    for i in range(1, chips):
        e = lax.bitwise_xor(chip, i)
        table[pl.ds(e, 1), pl.ds(core, 1)] = parts[2 * i - 2][...][None, None]
        table[pl.ds(e, 1), pl.ds(1 - core, 1)] = parts[2 * i - 1][...][None, None]
    order = list(range(chips))[:: -1 if backward else 1]
    carried[order[0]] = jnp.zeros(carried.shape[1:], F32)
    value = None
    for at, e in enumerate(order[:-1]):
        block = table[e].reshape(2 * cols, -1)
        if value is None:
            value = block[:, cols:]
        else:
            value = product(halves(real_form(block[:, :cols])), value) + block[:, cols:]
        carried[order[at + 1]] = value
    return carried[chip]


def incoming_scratch(chips, size, lanes):
    return [pltpu.VMEM((chips, 2, size // 2, lanes), F32), pltpu.VMEM((chips, size, lanes - size // 2), F32)]


def finish(near, offsets, maps, sources, mine, other, blocks, backward, following=(), joined=None, after=()):
    high, low = maps
    segs, _, coils, lines, width = sources.shape
    _, rows, size = high.shape
    cols, lanes = size // 2, mine.shape[1]
    chips = (len(blocks) + 1) // 2
    n = lax.axis_size("coil")
    own_coils = coils // n
    extra = list(following) + ([] if joined is None else [joined])

    def body(off_ref, hi_ref, lo_ref, m_ref, a_ref, b_ref, own, *refs):
        at = 2 * chips - 2
        rest, extra_refs, refs = refs[:at], refs[at : at + len(extra)], refs[at + len(extra) :]
        outs, refs = refs[:n], refs[n:]
        if following:
            e_ref, refs = refs[0], refs[1:]
        whole, table, carried, state, picked = refs
        choose = functools.partial(pick, state=state, picked=picked, offsets=off_ref, coils=coils)
        value = incoming(own, rest, table, carried, backward)
        moved = product(halves(real_form(b_ref[:, :cols])), value) + b_ref[:, cols:]
        value = jnp.where(my_chip()[1] == (1 if backward else 0), value, moved)
        source = [m_ref[s].reshape(rows, width) for s in range(segs)]
        states, _ = walk(lambda s: (hi_ref[s], lo_ref[s]), value, source, choose, backward)
        if following:
            e_ref[...] = response(extra_refs[0], extra_refs[1], states, choose, not backward)
        for s in range(segs):
            whole[s] = states[s].reshape(2, coils, lines, width)
        for i in range(n):
            cut = whole[:, :, pl.ds(spot(near, i) * own_coils, own_coils)]
            if joined is not None and i == 1:
                outs[i][0] = extra_refs[-1][...]
                outs[i][1] = cut
            else:
                outs[i][...] = cut

    block = (segs, 2, own_coils, lines, width)
    out_shape = [((2, *block) if joined is not None and i == 1 else block, F32) for i in range(n)]
    scratch = [pltpu.VMEM(sources.shape, F32)]
    if following:
        out_shape += [((size, lanes), F32), (sources.shape, F32)]
        scratch = []
    return call(
        body,
        "finish_backward" if backward else "finish_forward",
        out_shape,
        [VMEM] * (6 + len(blocks) + len(extra)),
        scratch
        + incoming_scratch(chips, size, lanes)
        + pick_scratch(lanes if following else width, rows, size),
        after=after,
    )(offsets, high, low, sources, mine, other, *blocks, *extra)


def unpack(forward, result, joined):
    n = len(forward)
    segs, parts, coils, lines, width = forward[0].shape
    sent = [forward[0], result[0], joined] + [b for i in range(2, n) for b in (forward[i], result[i])]

    def body(*refs):
        ins, outs, sems = refs[: len(sent)], refs[len(sent) : len(sent) + 2], refs[len(sent) + 2]
        copies = []
        for i in range(n):
            start = pl.multiple_of(spot(True, i) * width, width)
            for o in range(2):
                source = ins[2].at[o] if i == 1 else ins[o if i == 0 else 2 * i - 1 + o]
                copies.append(pltpu.make_async_copy(source, outs[o].at[:, :, :, :, pl.ds(start, width)], sems.at[i, o]))
        for c in copies:
            c.start()
        for c in copies:
            c.wait()

    return call(
        body,
        "unpack",
        [((segs, parts, coils, lines, n * width), F32)] * 2,
        [VMEM] * len(sent),
        [pltpu.SemaphoreType.DMA((n, 2))],
        [ANY] * 2,
    )(*sent)


def swap(block, axis, distance):
    return lax.ppermute(block, axis, [(i, i ^ distance) for i in range(lax.axis_size(axis))])


def spread_kernels(own):
    n = lax.axis_size("coil")
    blocks = {0: own}
    distance = n // 2
    while distance:
        blocks.update({i ^ distance: swap(blocks[i], "coil", distance) for i in sorted(blocks)})
        distance //= 2
    return [blocks[i] for i in range(n)]


def exchange(whole, half, first=None):
    chips = lax.axis_size("seg") // 2
    blocks = [whole]
    for i in range(1, chips):
        block = swap(half, "seg", 2 * i)
        if i == min(2, chips - 1) and first is not None:
            (block,) = hold(first, block)
        blocks += [block, swap(block, "seg", 1)]
    return blocks


def shards(measured, forward_kernel, backward_kernel, line_offsets):
    n = lax.axis_size("coil")
    places = lax.axis_size("seg")
    taps = line_offsets.shape[2]
    width = measured.shape[4] // n
    cols = forward_kernel.shape[3] * n
    first, last = line_offsets[0, 0], line_offsets[-1, 1]
    kernels_f, kernels_b = (jnp.swapaxes(k, 2, 3) for k in (forward_kernel, backward_kernel))
    aligned = width % LANES == 0 and (cols // taps // n) % 8 == 0
    if aligned:
        forward_blocks = spread_kernels(kernels_f)
        backward_blocks = spread_kernels(kernels_b)
        pieces = pack(measured)
        lines_blocks = [pieces[0]] + [swap(pieces[i], "coil", i) for i in range(1, n)]
        first, last = hold(forward_blocks[1], first, last)
    else:
        forward_blocks = list(lax.all_gather(kernels_f, "coil"))
        backward_blocks = list(lax.all_gather(kernels_b, "coil"))
        split = lax.all_to_all(measured, "coil", split_axis=4, concat_axis=2, tiled=True)
        split = jnp.pad(split, [(0, 0)] * 4 + [(0, -width % LANES)])
        lines_blocks = jnp.split(split, n, axis=2)
    after = lax.ppermute(first, "seg", [(i + 1, i) for i in range(places - 1)])[None]
    before = lax.ppermute(last, "seg", [(i, i + 1) for i in range(places - 1)])[None]
    offsets = jnp.concatenate([line_offsets[:, 0], line_offsets[:, 1], after, before])
    offsets = jnp.pad(offsets, [(0, -offsets.shape[0] % 8), (0, LANES - taps)])

    forward_maps = prepare(aligned, forward_blocks, False)
    lines = gather(aligned, lines_blocks, forward_maps[:1])
    backward_maps = prepare(aligned, backward_blocks, True)
    mine = summary(offsets, forward_maps, lines)
    other = swap(mine, "seg", 1)
    blocks = exchange(*compose(mine, other, cols, False))
    *forward_out, mine, forward = finish(aligned, offsets, forward_maps, lines, mine, other, blocks, False, backward_maps)
    other = swap(mine, "seg", 1)
    whole, half = compose(mine, other, cols, True)
    if aligned:
        home = dict(enumerate(forward_out[:2])) | {i: swap(forward_out[i], "coil", i) for i in range(2, n)}
        blocks = exchange(whole, half, home[n - 1] if n > 2 else None)
        result_out = finish(
            aligned,
            offsets,
            backward_maps,
            forward,
            mine,
            other,
            blocks,
            True,
            joined=forward_out[1],
            after=[home[i] for i in range(2, n - 1)],
        )
        result_home = [result_out[0]] + [swap(result_out[i], "coil", i) for i in range(1, n)]
        return tuple(unpack(home, result_home, result_home[1]))
    blocks = exchange(whole, half)
    result_out = finish(aligned, offsets, backward_maps, forward, mine, other, blocks, True)

    def rejoin(blocks):
        states = lax.all_to_all(jnp.stack(blocks), "coil", split_axis=0, concat_axis=0)[..., :width]
        states = jnp.moveaxis(states, 0, 4)
        return states.reshape(states.shape[:4] + (n * width,))

    return rejoin(forward_out), rejoin(result_out)


def solution(mesh):
    placed = (
        P("seg", None, "coil", None, None),
        P("seg", None, None, "coil"),
        P("seg", None, None, "coil"),
        P("seg", None, None),
    )
    return jax.shard_map(
        shards,
        mesh=mesh,
        in_specs=placed,
        out_specs=(P("seg", None, "coil", None, None), P("seg", None, "coil", None, None)),
        check_vma=False,
    )
```

```python
import functools

import jax
import jax.numpy as jnp
from jax import lax
from jax.experimental import pallas as pl
from jax.experimental.pallas import tpu as pltpu
from jax.sharding import PartitionSpec as P

F32 = jnp.float32
BF16 = jnp.bfloat16
VMEM = pl.BlockSpec(memory_space=pltpu.VMEM)
ANY = pl.BlockSpec(memory_space=pl.ANY)
HBM = pl.BlockSpec(memory_space=pltpu.HBM)
LANES = 128
PARAMS = pltpu.CompilerParams(vmem_limit_bytes=40 * 2**20)


def call(body, name, out_shape, in_specs, scratch=(), out_specs=None, after=()):
    def whole(*refs):
        body(*refs[len(after) :])

    kernel = pl.pallas_call(
        whole,
        out_shape=[jax.ShapeDtypeStruct(shape, dtype) for shape, dtype in out_shape],
        in_specs=[ANY] * len(after) + in_specs,
        out_specs=out_specs or [VMEM] * len(out_shape),
        scratch_shapes=list(scratch),
        compiler_params=PARAMS,
        name=name,
    )
    return functools.partial(kernel, *after)


def halves(a):
    high = a.astype(BF16)
    return high, (a - high.astype(F32)).astype(BF16)


def product(left, right):
    dot = functools.partial(jnp.dot, preferred_element_type=F32)
    high, low = left
    other_high, other_low = halves(right)
    width = right.shape[1]
    if width > LANES:
        return dot(high, other_high) + (dot(high, other_low) + dot(low, other_high))
    both = dot(high, jnp.concatenate([other_high, other_low], axis=1))
    return both[:, :width] + (both[:, width:] + dot(low, other_high))


def real_form(columns):
    size = columns.shape[0] // 2
    return jnp.concatenate([columns, jnp.concatenate([-columns[size:], columns[:size]], axis=0)], axis=1)


def pick(value, state, picked, offsets, coils, row):
    taps, lines = picked.shape[1] // 2 // coils, state.shape[1] // 2 // coils
    line = [jnp.sum(offsets[row : row + 1, tap : tap + 1]) for tap in range(taps)]
    chunks = value.shape[1] // LANES
    for i in range(chunks):
        state[i] = value[:, i * LANES : (i + 1) * LANES]
        for part in range(2):
            for tap in range(taps):
                source = pl.ds(part * coils * lines + line[tap], coils, stride=lines)
                picked[i, pl.ds(part * coils * taps + tap, coils, stride=taps), :] = state[i, source, :]
    return jnp.concatenate([picked[i] for i in range(chunks)], axis=1)


def pick_scratch(lanes, state, size):
    return [pltpu.VMEM((lanes // LANES, state, LANES), F32), pltpu.VMEM((lanes // LANES, size, LANES), F32)]


def visits(segs, backward):
    if backward:
        return [(s, segs + s - 1 if s else 2 * segs + 1) for s in reversed(range(segs))]
    return [(s, s + 1 if s < segs - 1 else 2 * segs) for s in range(segs)]


def walk(maps, carried, sources, choose, backward, sends):
    states = list(sources)
    order = visits(len(sources), backward)
    for s, row in order:
        if carried is not None:
            states[s] = product(maps(s), carried) + sources[s]
        if sends or s != order[-1][0]:
            carried = choose(states[s], row=row)
    return carried if sends else states


def response(high, low, states, choose, backward):
    size = high.shape[2]
    first = visits(len(states), backward)[0][0]
    columns = high[first, :, : size // 2].astype(F32) + low[first, :, : size // 2].astype(F32)
    blank = jnp.zeros_like(columns)
    sources = [jnp.concatenate([columns if s == first else blank, state], axis=1) for s, state in enumerate(states)]
    return walk(lambda s: (high[s], low[s]), None, sources, choose, backward, True)


def spot(near, i):
    return lax.bitwise_xor(lax.axis_index("coil"), i) if near else i


def my_chip():
    seg = lax.axis_index("seg")
    return lax.shift_right_logical(seg, 1), lax.bitwise_and(seg, 1)


def pack(measured):
    segs, parts, coils, lines, samples = measured.shape
    n = lax.axis_size("coil")
    width = samples // n

    def body(m_ref, *rest):
        outs, sems = rest[:n], rest[n]
        copies = []
        for i in range(n):
            start = pl.multiple_of(spot(True, i) * width, width)
            copies.append(pltpu.make_async_copy(m_ref.at[:, :, :, :, pl.ds(start, width)], outs[i], sems.at[i]))
        for c in copies:
            c.start()
        for c in copies:
            c.wait()

    out = ((segs, parts, coils, lines, width), F32)
    return call(body, "pack", [out] * n, [HBM], [pltpu.SemaphoreType.DMA((n,))])(measured)


def hold(first, *values):
    def body(_, *refs):
        for i in range(len(values)):
            refs[len(values) + i][...] = refs[i][...]

    out_shape = [(v.shape, v.dtype) for v in values]
    return call(body, "hold", out_shape, [ANY] + [VMEM] * len(values))(first, *values)


def gather(near, blocks, after):
    n = len(blocks)
    segs, parts, coils, lines, width = blocks[0].shape

    def body(*refs):
        for i in range(n):
            refs[n][:, :, pl.ds(spot(near, i) * coils, coils)] = refs[i][...]

    out = ((segs, parts, n * coils, lines, width), F32)
    return call(body, "gather", [out], [VMEM] * n, after=after)(*blocks)[0]


def prepare(near, blocks, backward):
    n = len(blocks)
    segs, _, block_cols, rows = blocks[0].shape
    cols = block_cols * n
    size = 2 * cols

    def body(*refs):
        hi_ref, lo_ref, kt = refs[n:]
        for i in range(n):
            kt[:, :, pl.ds(spot(near, i), 1)] = refs[i][...][:, :, None]
        for s in range(segs):
            real, imag = (kt[s, part].reshape(cols, rows).T for part in range(2))
            hi_ref[s], lo_ref[s] = halves(real_form(jnp.concatenate([real, imag], axis=0)))

    return call(
        body,
        "prepare_backward" if backward else "prepare_forward",
        [((segs, 2 * rows, size), BF16)] * 2,
        [VMEM] * n,
        [pltpu.VMEM((segs, 2, n, block_cols, rows), F32)],
    )(*blocks)


def summary(offsets, maps, sources, backward):
    high, low = maps
    _, rows, size = high.shape
    segs, _, coils, _, width = sources.shape
    lanes = size // 2 + width

    def body(off_ref, hi_ref, lo_ref, m_ref, e_ref, state, picked):
        choose = functools.partial(pick, state=state, picked=picked, offsets=off_ref, coils=coils)
        e_ref[...] = response(hi_ref, lo_ref, [m_ref[s].reshape(rows, width) for s in range(segs)], choose, backward)

    return call(
        body,
        "summary_backward" if backward else "summary_forward",
        [((size, lanes), F32)],
        [VMEM] * 4,
        pick_scratch(lanes, rows, size),
    )(offsets, high, low, sources)[0]


def compose(mine, other, cols, backward):
    size, lanes = mine.shape

    def body(a_ref, b_ref, whole, out_ref, pair):
        _, core = my_chip()
        pair[pl.ds(core, 1)] = a_ref[...][None]
        pair[pl.ds(1 - core, 1)] = b_ref[...][None]
        near, far = (pair[1], pair[0]) if backward else (pair[0], pair[1])
        both = product(halves(real_form(far[:, :cols])), near)
        whole[:, :cols] = both[:, :cols]
        whole[:, cols:] = both[:, cols:] + far[:, cols:]
        out_ref[...] = whole[pl.ds(pl.multiple_of(core * (size // 2), size // 2), size // 2), :]

    return call(
        body,
        "compose_backward" if backward else "compose_forward",
        [((size, lanes), F32), ((size // 2, lanes), F32)],
        [VMEM, VMEM],
        [pltpu.VMEM((2, size, lanes), F32)],
    )(mine, other)


def incoming(own, parts, table, carried, backward):
    chips, _, cols, _ = table.shape
    chip, core = my_chip()
    table[pl.ds(chip, 1)] = own[...].reshape((1,) + table.shape[1:])
    for i in range(1, chips):
        e = lax.bitwise_xor(chip, i)
        table[pl.ds(e, 1), pl.ds(core, 1)] = parts[2 * i - 2][...][None, None]
        table[pl.ds(e, 1), pl.ds(1 - core, 1)] = parts[2 * i - 1][...][None, None]
    order = list(range(chips))[:: -1 if backward else 1]
    carried[order[0]] = jnp.zeros(carried.shape[1:], F32)
    value = None
    for at, e in enumerate(order[:-1]):
        block = table[e].reshape(2 * cols, -1)
        if value is None:
            value = block[:, cols:]
        else:
            value = product(halves(real_form(block[:, :cols])), value) + block[:, cols:]
        carried[order[at + 1]] = value
    return carried[chip]


def incoming_scratch(chips, size, lanes):
    return [pltpu.VMEM((chips, 2, size // 2, lanes), F32), pltpu.VMEM((chips, size, lanes - size // 2), F32)]


def finish(near, offsets, maps, sources, mine, other, blocks, backward, joined=None, after=()):
    high, low = maps
    segs, _, coils, lines, width = sources.shape
    _, rows, size = high.shape
    cols, lanes = size // 2, mine.shape[1]
    chips = (len(blocks) + 1) // 2
    n = lax.axis_size("coil")
    own_coils = coils // n
    extra = [] if joined is None else [joined]

    def body(off_ref, hi_ref, lo_ref, m_ref, a_ref, b_ref, own, *refs):
        at = 2 * chips - 2
        rest, extra_refs, refs = refs[:at], refs[at : at + len(extra)], refs[at + len(extra) :]
        pieces = n if backward else 0
        outs, refs = refs[:pieces], refs[pieces:]
        whole, table, carried, state, picked = refs
        choose = functools.partial(pick, state=state, picked=picked, offsets=off_ref, coils=coils)
        value = incoming(own, rest, table, carried, backward)
        moved = product(halves(real_form(b_ref[:, :cols])), value) + b_ref[:, cols:]
        value = jnp.where(my_chip()[1] == (1 if backward else 0), value, moved)
        source = [m_ref[s].reshape(rows, width) for s in range(segs)]
        states = walk(lambda s: (hi_ref[s], lo_ref[s]), value, source, choose, backward, False)
        for s in range(segs):
            whole[s] = states[s].reshape(2, coils, lines, width)
        for i in range(len(outs)):
            cut = whole[:, :, pl.ds(spot(near, i) * own_coils, own_coils)]
            if joined is not None and i == 1:
                outs[i][0] = extra_refs[-1][...]
                outs[i][1] = cut
            else:
                outs[i][...] = cut

    block = (segs, 2, own_coils, lines, width)
    out_shape = [((2, *block) if joined is not None and i == 1 else block, F32) for i in range(n)]
    scratch = [pltpu.VMEM(sources.shape, F32)]
    if not backward:
        out_shape = [(sources.shape, F32)]
        scratch = []
    return call(
        body,
        "finish_backward" if backward else "finish_forward",
        out_shape,
        [VMEM] * (6 + len(blocks) + len(extra)),
        scratch + incoming_scratch(chips, size, lanes) + pick_scratch(width, rows, size),
        after=after,
    )(offsets, high, low, sources, mine, other, *blocks, *extra)


def cut(near, states, n, after):
    segs, parts, coils, lines, width = states.shape
    own_coils = coils // n

    def body(s_ref, *outs):
        for i in range(n):
            outs[i][...] = s_ref[:, :, pl.ds(spot(near, i) * own_coils, own_coils)]

    out = ((segs, parts, own_coils, lines, width), F32)
    return call(body, "cut", [out] * n, [VMEM], after=after)(states)


def unpack(forward, result, joined):
    n = len(forward)
    segs, parts, coils, lines, width = forward[0].shape
    sent = [forward[0], result[0], joined] + [b for i in range(2, n) for b in (forward[i], result[i])]

    def body(*refs):
        ins, outs, sems = refs[: len(sent)], refs[len(sent) : len(sent) + 2], refs[len(sent) + 2]
        copies = []
        for i in range(n):
            start = pl.multiple_of(spot(True, i) * width, width)
            for o in range(2):
                source = ins[2].at[o] if i == 1 else ins[o if i == 0 else 2 * i - 1 + o]
                copies.append(pltpu.make_async_copy(source, outs[o].at[:, :, :, :, pl.ds(start, width)], sems.at[i, o]))
        for c in copies:
            c.start()
        for c in copies:
            c.wait()

    return call(
        body,
        "unpack",
        [((segs, parts, coils, lines, n * width), F32)] * 2,
        [VMEM] * len(sent),
        [pltpu.SemaphoreType.DMA((n, 2))],
        [ANY] * 2,
    )(*sent)


def swap(block, axis, distance):
    return lax.ppermute(block, axis, [(i, i ^ distance) for i in range(lax.axis_size(axis))])


def spread_kernels(own):
    n = lax.axis_size("coil")
    blocks = {0: own}
    distance = n // 2
    while distance:
        blocks.update({i ^ distance: swap(blocks[i], "coil", distance) for i in sorted(blocks)})
        distance //= 2
    return [blocks[i] for i in range(n)]


def exchange(whole, half, first=None):
    chips = lax.axis_size("seg") // 2
    blocks = [whole]
    for i in range(1, chips):
        block = swap(half, "seg", 2 * i)
        if i == min(2, chips - 1) and first is not None:
            (block,) = hold(first, block)
        blocks += [block, swap(block, "seg", 1)]
    return blocks


def shards(measured, forward_kernel, backward_kernel, line_offsets):
    n = lax.axis_size("coil")
    places = lax.axis_size("seg")
    taps = line_offsets.shape[2]
    width = measured.shape[4] // n
    cols = forward_kernel.shape[3] * n
    kernels_f, kernels_b = (jnp.swapaxes(k, 2, 3) for k in (forward_kernel, backward_kernel))
    aligned = width % LANES == 0 and (cols // taps // n) % 8 == 0
    if aligned:
        forward_blocks = spread_kernels(kernels_f)
        backward_blocks = spread_kernels(kernels_b)
        pieces = pack(measured)
        lines_blocks = [pieces[0]] + [swap(pieces[i], "coil", i) for i in range(1, n)]
    else:
        forward_blocks = list(lax.all_gather(kernels_f, "coil"))
        backward_blocks = list(lax.all_gather(kernels_b, "coil"))
        split = lax.all_to_all(measured, "coil", split_axis=4, concat_axis=2, tiled=True)
        split = jnp.pad(split, [(0, 0)] * 4 + [(0, -width % LANES)])
        lines_blocks = jnp.split(split, n, axis=2)
    after = lax.ppermute(line_offsets[0, 0], "seg", [((i + 1) % places, i) for i in range(places)])[None]
    before = lax.ppermute(line_offsets[-1, 1], "seg", [(i, (i + 1) % places) for i in range(places)])[None]
    offsets = jnp.concatenate([line_offsets[:, 0], line_offsets[:, 1], after, before])
    offsets = jnp.pad(offsets, [(0, -offsets.shape[0] % 8), (0, LANES - taps)])

    forward_maps = prepare(aligned, forward_blocks, False)
    lines = gather(aligned, lines_blocks, forward_maps[:1])
    backward_maps = prepare(aligned, backward_blocks, True)
    mine = summary(offsets, forward_maps, lines, False)
    other = swap(mine, "seg", 1)
    blocks = exchange(*compose(mine, other, cols, False))
    (forward,) = finish(aligned, offsets, forward_maps, lines, mine, other, blocks, False)
    forward_out = cut(aligned, forward, n, backward_maps[:1])
    mine = summary(offsets, backward_maps, forward, True)
    other = swap(mine, "seg", 1)
    whole, half = compose(mine, other, cols, True)
    if aligned:
        home = dict(enumerate(forward_out[:2])) | {i: swap(forward_out[i], "coil", i) for i in range(2, n)}
        blocks = exchange(whole, half, home[n - 1] if n > 2 else None)
        result_out = finish(
            aligned,
            offsets,
            backward_maps,
            forward,
            mine,
            other,
            blocks,
            True,
            joined=forward_out[1],
            after=[home[i] for i in range(2, n - 1)],
        )
        result_home = [result_out[0]] + [swap(result_out[i], "coil", i) for i in range(1, n)]
        return tuple(unpack(home, result_home, result_home[1]))
    blocks = exchange(whole, half)
    result_out = finish(aligned, offsets, backward_maps, forward, mine, other, blocks, True)

    def rejoin(blocks):
        states = lax.all_to_all(jnp.stack(blocks), "coil", split_axis=0, concat_axis=0)[..., :width]
        states = jnp.moveaxis(states, 0, 4)
        return states.reshape(states.shape[:4] + (n * width,))

    return rejoin(forward_out), rejoin(result_out)


def solution(mesh):
    placed = (
        P("seg", None, "coil", None, None),
        P("seg", None, None, "coil"),
        P("seg", None, None, "coil"),
        P("seg", None, None),
    )
    return jax.shard_map(
        shards,
        mesh=mesh,
        in_specs=placed,
        out_specs=(P("seg", None, "coil", None, None), P("seg", None, "coil", None, None)),
        check_vma=False,
    )
```

```python
import functools

import jax
import jax.numpy as jnp
from jax import lax
from jax.experimental import pallas as pl
from jax.experimental.pallas import tpu as pltpu
from jax.sharding import PartitionSpec as P

F32 = jnp.float32
BF16 = jnp.bfloat16
VMEM = pl.BlockSpec(memory_space=pltpu.VMEM)
ANY = pl.BlockSpec(memory_space=pl.ANY)
HBM = pl.BlockSpec(memory_space=pltpu.HBM)
LANES = 128
PARAMS = pltpu.CompilerParams(vmem_limit_bytes=40 * 2**20)


def call(body, name, out_shape, in_specs, scratch=(), out_specs=None, after=(), aliases=None):
    def whole(*refs):
        body(*refs[len(after) :])

    kernel = pl.pallas_call(
        whole,
        out_shape=[jax.ShapeDtypeStruct(shape, dtype) for shape, dtype in out_shape],
        in_specs=[ANY] * len(after) + in_specs,
        out_specs=out_specs or [VMEM] * len(out_shape),
        scratch_shapes=list(scratch),
        input_output_aliases=aliases or {},
        compiler_params=PARAMS,
        name=name,
    )
    return functools.partial(kernel, *after)


def halves(a):
    high = a.astype(BF16)
    return high, (a - high.astype(F32)).astype(BF16)


def product(left, right):
    dot = functools.partial(jnp.dot, preferred_element_type=F32)
    high, low = left
    other_high, other_low = halves(right)
    width = right.shape[1]
    if width > LANES:
        return dot(high, other_high) + (dot(high, other_low) + dot(low, other_high))
    both = dot(high, jnp.concatenate([other_high, other_low], axis=1))
    return both[:, :width] + (both[:, width:] + dot(low, other_high))


def real_form(columns):
    size = columns.shape[0] // 2
    return jnp.concatenate([columns, jnp.concatenate([-columns[size:], columns[:size]], axis=0)], axis=1)


def pick(value, state, picked, offsets, coils, row):
    taps, lines = picked.shape[1] // 2 // coils, state.shape[1] // 2 // coils
    line = [jnp.sum(offsets[row : row + 1, tap : tap + 1]) for tap in range(taps)]
    chunks = value.shape[1] // LANES
    for i in range(chunks):
        state[i] = value[:, i * LANES : (i + 1) * LANES]
        for part in range(2):
            for tap in range(taps):
                source = pl.ds(part * coils * lines + line[tap], coils, stride=lines)
                picked[i, pl.ds(part * coils * taps + tap, coils, stride=taps), :] = state[i, source, :]
    return jnp.concatenate([picked[i] for i in range(chunks)], axis=1)


def pick_scratch(lanes, state, size):
    return [pltpu.VMEM((lanes // LANES, state, LANES), F32), pltpu.VMEM((lanes // LANES, size, LANES), F32)]


def visits(segs, backward):
    if backward:
        return [(s, segs + s - 1 if s else 2 * segs + 1) for s in reversed(range(segs))]
    return [(s, s + 1 if s < segs - 1 else 2 * segs) for s in range(segs)]


def walk(maps, carried, sources, choose, backward, sends):
    states = list(sources)
    order = visits(len(sources), backward)
    for s, row in order:
        if carried is not None:
            states[s] = product(maps(s), carried) + sources[s]
        if sends or s != order[-1][0]:
            carried = choose(states[s], row=row)
    return carried if sends else states


def response(high, low, states, choose, backward):
    size = high.shape[2]
    first = visits(len(states), backward)[0][0]
    columns = high[first, :, : size // 2].astype(F32) + low[first, :, : size // 2].astype(F32)
    blank = jnp.zeros_like(columns)
    sources = [jnp.concatenate([columns if s == first else blank, state], axis=1) for s, state in enumerate(states)]
    return walk(lambda s: (high[s], low[s]), None, sources, choose, backward, True)


def spot(near, i):
    return lax.bitwise_xor(lax.axis_index("coil"), i) if near else i


def my_chip():
    seg = lax.axis_index("seg")
    return lax.shift_right_logical(seg, 1), lax.bitwise_and(seg, 1)


def pack(measured):
    segs, parts, coils, lines, samples = measured.shape
    n = lax.axis_size("coil")
    width = samples // n

    def body(m_ref, *rest):
        outs, sems = rest[:n], rest[n]
        copies = []
        for i in range(n):
            start = pl.multiple_of(spot(True, i) * width, width)
            copies.append(pltpu.make_async_copy(m_ref.at[:, :, :, :, pl.ds(start, width)], outs[i], sems.at[i]))
        for c in copies:
            c.start()
        for c in copies:
            c.wait()

    out = ((segs, parts, coils, lines, width), F32)
    return call(body, "pack", [out] * n, [HBM], [pltpu.SemaphoreType.DMA((n,))])(measured)


def hold(first, *values):
    def body(_, *refs):
        for i in range(len(values)):
            refs[len(values) + i][...] = refs[i][...]

    out_shape = [(v.shape, v.dtype) for v in values]
    return call(body, "hold", out_shape, [ANY] + [VMEM] * len(values))(first, *values)


def gather(near, blocks, after):
    n = len(blocks)
    segs, parts, coils, lines, width = blocks[0].shape

    def body(*refs):
        for i in range(n):
            refs[n][:, :, pl.ds(spot(near, i) * coils, coils)] = refs[i][...]

    out = ((segs, parts, n * coils, lines, width), F32)
    return call(body, "gather", [out], [VMEM] * n, after=after)(*blocks)[0]


def prepare(near, blocks, backward):
    n = len(blocks)
    segs, _, block_cols, rows = blocks[0].shape
    cols = block_cols * n
    size = 2 * cols

    def body(*refs):
        hi_ref, lo_ref, kt = refs[n:]
        for i in range(n):
            kt[:, :, pl.ds(spot(near, i), 1)] = refs[i][...][:, :, None]
        for s in range(segs):
            real, imag = (kt[s, part].reshape(cols, rows).T for part in range(2))
            hi_ref[s], lo_ref[s] = halves(real_form(jnp.concatenate([real, imag], axis=0)))

    return call(
        body,
        "prepare_backward" if backward else "prepare_forward",
        [((segs, 2 * rows, size), BF16)] * 2,
        [VMEM] * n,
        [pltpu.VMEM((segs, 2, n, block_cols, rows), F32)],
    )(*blocks)


def summary(offsets, maps, sources, backward):
    high, low = maps
    _, rows, size = high.shape
    segs, _, coils, _, width = sources.shape
    lanes = size // 2 + width

    def body(off_ref, hi_ref, lo_ref, m_ref, e_ref, state, picked):
        choose = functools.partial(pick, state=state, picked=picked, offsets=off_ref, coils=coils)
        e_ref[...] = response(hi_ref, lo_ref, [m_ref[s].reshape(rows, width) for s in range(segs)], choose, backward)

    return call(
        body,
        "summary_backward" if backward else "summary_forward",
        [((size, lanes), F32)],
        [VMEM] * 4,
        pick_scratch(lanes, rows, size),
    )(offsets, high, low, sources)[0]


def compose(mine, other, cols, backward):
    size, lanes = mine.shape

    def body(a_ref, b_ref, whole, out_ref, pair):
        _, core = my_chip()
        pair[pl.ds(core, 1)] = a_ref[...][None]
        pair[pl.ds(1 - core, 1)] = b_ref[...][None]
        near, far = (pair[1], pair[0]) if backward else (pair[0], pair[1])
        both = product(halves(real_form(far[:, :cols])), near)
        whole[:, :cols] = both[:, :cols]
        whole[:, cols:] = both[:, cols:] + far[:, cols:]
        out_ref[...] = whole[pl.ds(pl.multiple_of(core * (size // 2), size // 2), size // 2), :]

    return call(
        body,
        "compose_backward" if backward else "compose_forward",
        [((size, lanes), F32), ((size // 2, lanes), F32)],
        [VMEM, VMEM],
        [pltpu.VMEM((2, size, lanes), F32)],
    )(mine, other)


def incoming(own, parts, table, carried, backward):
    chips, _, cols, _ = table.shape
    chip, core = my_chip()
    table[pl.ds(chip, 1)] = own[...].reshape((1,) + table.shape[1:])
    for i in range(1, chips):
        e = lax.bitwise_xor(chip, i)
        table[pl.ds(e, 1), pl.ds(core, 1)] = parts[2 * i - 2][...][None, None]
        table[pl.ds(e, 1), pl.ds(1 - core, 1)] = parts[2 * i - 1][...][None, None]
    order = list(range(chips))[:: -1 if backward else 1]
    carried[order[0]] = jnp.zeros(carried.shape[1:], F32)
    value = None
    for at, e in enumerate(order[:-1]):
        block = table[e].reshape(2 * cols, -1)
        if value is None:
            value = block[:, cols:]
        else:
            value = product(halves(real_form(block[:, :cols])), value) + block[:, cols:]
        carried[order[at + 1]] = value
    return carried[chip]


def incoming_scratch(chips, size, lanes):
    return [pltpu.VMEM((chips, 2, size // 2, lanes), F32), pltpu.VMEM((chips, size, lanes - size // 2), F32)]


def finish(near, offsets, maps, sources, mine, other, blocks, backward, joined=None, after=()):
    high, low = maps
    segs, _, coils, lines, width = sources.shape
    _, rows, size = high.shape
    cols, lanes = size // 2, mine.shape[1]
    chips = (len(blocks) + 1) // 2
    n = lax.axis_size("coil")
    own_coils = coils // n
    extra = [] if joined is None else [joined]

    def body(off_ref, hi_ref, lo_ref, m_ref, a_ref, b_ref, own, *refs):
        at = 2 * chips - 2
        rest, extra_refs, refs = refs[:at], refs[at : at + len(extra)], refs[at + len(extra) :]
        pieces = n if backward else 0
        outs, refs = refs[:pieces], refs[pieces:]
        whole, table, carried, state, picked = refs
        choose = functools.partial(pick, state=state, picked=picked, offsets=off_ref, coils=coils)
        value = incoming(own, rest, table, carried, backward)
        moved = product(halves(real_form(b_ref[:, :cols])), value) + b_ref[:, cols:]
        value = jnp.where(my_chip()[1] == (1 if backward else 0), value, moved)
        source = [m_ref[s].reshape(rows, width) for s in range(segs)]
        states = walk(lambda s: (hi_ref[s], lo_ref[s]), value, source, choose, backward, False)
        for s in range(segs):
            whole[s] = states[s].reshape(2, coils, lines, width)
        for i in range(len(outs)):
            cut = whole[:, :, pl.ds(spot(near, i) * own_coils, own_coils)]
            if joined is not None and i == 1:
                outs[i][0] = extra_refs[-1][...]
                outs[i][1] = cut
            else:
                outs[i][...] = cut

    block = (segs, 2, own_coils, lines, width)
    out_shape = [((2, *block) if joined is not None and i == 1 else block, F32) for i in range(n)]
    scratch = [pltpu.VMEM(sources.shape, F32)]
    if not backward:
        out_shape = [(sources.shape, F32)]
        scratch = []
    return call(
        body,
        "finish_backward" if backward else "finish_forward",
        out_shape,
        [VMEM] * (6 + len(blocks) + len(extra)),
        scratch + incoming_scratch(chips, size, lanes) + pick_scratch(width, rows, size),
        after=after,
    )(offsets, high, low, sources, mine, other, *blocks, *extra)


def cut(near, states, n, after):
    segs, parts, coils, lines, width = states.shape
    own_coils = coils // n

    def body(s_ref, *outs):
        for i in range(n):
            outs[i][...] = s_ref[:, :, pl.ds(spot(near, i) * own_coils, own_coils)]

    out = ((segs, parts, own_coils, lines, width), F32)
    return call(body, "cut", [out] * n, [VMEM], after=after)(states)


def unpack(blocks, begun=()):
    n = lax.axis_size("coil")
    arrays, places = [], []
    for i, pair in blocks:
        for o in range(2):
            if isinstance(pair, tuple):
                if pair[o] is None:
                    continue
                places.append((len(arrays), i, o, False))
                arrays.append(pair[o])
            else:
                places.append((len(arrays), i, o, True))
        if not isinstance(pair, tuple):
            arrays.append(pair)
    segs, parts, coils, lines, width = arrays[0].shape[-5:]

    def body(*refs):
        ins, outs, sems = refs[len(begun) :], refs[len(begun) + len(arrays) :], refs[-1]
        copies = []
        for k, (at, i, o, joined) in enumerate(places):
            start = pl.multiple_of(spot(True, i) * width, width)
            source = ins[at].at[o] if joined else ins[at]
            copies.append(pltpu.make_async_copy(source, outs[o].at[:, :, :, :, pl.ds(start, width)], sems.at[k]))
        for c in copies:
            c.start()
        for c in copies:
            c.wait()

    return call(
        body,
        "unpack_rest" if begun else "unpack",
        [((segs, parts, coils, lines, n * width), F32)] * 2,
        [ANY] * len(begun) + [VMEM] * len(arrays),
        [pltpu.SemaphoreType.DMA((len(places),))],
        [ANY] * 2,
        aliases={i: i for i in range(len(begun))},
    )(*begun, *arrays)


def swap(block, axis, distance):
    return lax.ppermute(block, axis, [(i, i ^ distance) for i in range(lax.axis_size(axis))])


def spread_kernels(own):
    n = lax.axis_size("coil")
    blocks = {0: own}
    distance = n // 2
    while distance:
        blocks.update({i ^ distance: swap(blocks[i], "coil", distance) for i in sorted(blocks)})
        distance //= 2
    return [blocks[i] for i in range(n)]


def exchange(whole, half, first=None):
    chips = lax.axis_size("seg") // 2
    blocks = [whole]
    for i in range(1, chips):
        block = swap(half, "seg", 2 * i)
        if i == min(2, chips - 1) and first is not None:
            (block,) = hold(first, block)
        blocks += [block, swap(block, "seg", 1)]
    return blocks


def shards(measured, forward_kernel, backward_kernel, line_offsets):
    n = lax.axis_size("coil")
    places = lax.axis_size("seg")
    taps = line_offsets.shape[2]
    width = measured.shape[4] // n
    cols = forward_kernel.shape[3] * n
    kernels_f, kernels_b = (jnp.swapaxes(k, 2, 3) for k in (forward_kernel, backward_kernel))
    aligned = width % LANES == 0 and (cols // taps // n) % 8 == 0
    if aligned:
        forward_blocks = spread_kernels(kernels_f)
        backward_blocks = spread_kernels(kernels_b)
        pieces = pack(measured)
        lines_blocks = [pieces[0]] + [swap(pieces[i], "coil", i) for i in range(1, n)]
    else:
        forward_blocks = list(lax.all_gather(kernels_f, "coil"))
        backward_blocks = list(lax.all_gather(kernels_b, "coil"))
        split = lax.all_to_all(measured, "coil", split_axis=4, concat_axis=2, tiled=True)
        split = jnp.pad(split, [(0, 0)] * 4 + [(0, -width % LANES)])
        lines_blocks = jnp.split(split, n, axis=2)
    after = lax.ppermute(line_offsets[0, 0], "seg", [((i + 1) % places, i) for i in range(places)])[None]
    before = lax.ppermute(line_offsets[-1, 1], "seg", [(i, (i + 1) % places) for i in range(places)])[None]
    offsets = jnp.concatenate([line_offsets[:, 0], line_offsets[:, 1], after, before])
    offsets = jnp.pad(offsets, [(0, -offsets.shape[0] % 8), (0, LANES - taps)])

    forward_maps = prepare(aligned, forward_blocks, False)
    lines = gather(aligned, lines_blocks, forward_maps[:1])
    backward_maps = prepare(aligned, backward_blocks, True)
    mine = summary(offsets, forward_maps, lines, False)
    other = swap(mine, "seg", 1)
    blocks = exchange(*compose(mine, other, cols, False))
    (forward,) = finish(aligned, offsets, forward_maps, lines, mine, other, blocks, False)
    forward_out = cut(aligned, forward, n, backward_maps[:1])
    mine = summary(offsets, backward_maps, forward, True)
    other = swap(mine, "seg", 1)
    whole, half = compose(mine, other, cols, True)
    if aligned:
        home = dict(enumerate(forward_out[:2])) | {i: swap(forward_out[i], "coil", i) for i in range(2, n)}
        blocks = exchange(whole, half, home[n - 1] if n > 2 else None)
        result_out = finish(
            aligned,
            offsets,
            backward_maps,
            forward,
            mine,
            other,
            blocks,
            True,
            joined=forward_out[1],
            after=[home[i] for i in range(2, n - 1)],
        )
        result_home = [result_out[0]] + [swap(result_out[i], "coil", i) for i in range(1, n)]
        begun = unpack([(0, (home[0], result_out[0]))] + [(i, (home[i], None)) for i in range(2, n)])
        for i in range(1, n):
            begun = unpack([(i, (None, result_home[i]) if i > 1 else result_home[i])], begun)
        return tuple(begun)
    blocks = exchange(whole, half)
    result_out = finish(aligned, offsets, backward_maps, forward, mine, other, blocks, True)

    def rejoin(blocks):
        states = lax.all_to_all(jnp.stack(blocks), "coil", split_axis=0, concat_axis=0)[..., :width]
        states = jnp.moveaxis(states, 0, 4)
        return states.reshape(states.shape[:4] + (n * width,))

    return rejoin(forward_out), rejoin(result_out)


def solution(mesh):
    placed = (
        P("seg", None, "coil", None, None),
        P("seg", None, None, "coil"),
        P("seg", None, None, "coil"),
        P("seg", None, None),
    )
    return jax.shard_map(
        shards,
        mesh=mesh,
        in_specs=placed,
        out_specs=(P("seg", None, "coil", None, None), P("seg", None, "coil", None, None)),
        check_vma=False,
    )
```

```python
import functools

import jax
import jax.numpy as jnp
from jax import lax
from jax.experimental import pallas as pl
from jax.experimental.pallas import tpu as pltpu
from jax.sharding import PartitionSpec as P

F32 = jnp.float32
BF16 = jnp.bfloat16
VMEM = pl.BlockSpec(memory_space=pltpu.VMEM)
ANY = pl.BlockSpec(memory_space=pl.ANY)
HBM = pl.BlockSpec(memory_space=pltpu.HBM)
LANES = 128
PARAMS = pltpu.CompilerParams(vmem_limit_bytes=40 * 2**20)


def call(body, name, out_shape, in_specs, scratch=(), out_specs=None, after=(), aliases=None):
    def whole(*refs):
        body(*refs[len(after) :])

    kernel = pl.pallas_call(
        whole,
        out_shape=[jax.ShapeDtypeStruct(shape, dtype) for shape, dtype in out_shape],
        in_specs=[ANY] * len(after) + in_specs,
        out_specs=out_specs or [VMEM] * len(out_shape),
        scratch_shapes=list(scratch),
        input_output_aliases=aliases or {},
        compiler_params=PARAMS,
        name=name,
    )
    return functools.partial(kernel, *after)


def halves(a):
    high = a.astype(BF16)
    return high, (a - high.astype(F32)).astype(BF16)


def product(left, right):
    dot = functools.partial(jnp.dot, preferred_element_type=F32)
    high, low = left
    other_high, other_low = halves(right)
    width = right.shape[1]
    if width > LANES:
        return dot(high, other_high) + (dot(high, other_low) + dot(low, other_high))
    both = dot(high, jnp.concatenate([other_high, other_low], axis=1))
    return both[:, :width] + (both[:, width:] + dot(low, other_high))


def real_form(columns):
    size = columns.shape[0] // 2
    return jnp.concatenate([columns, jnp.concatenate([-columns[size:], columns[:size]], axis=0)], axis=1)


def pick(value, state, picked, offsets, coils, row):
    taps, lines = picked.shape[1] // 2 // coils, state.shape[1] // 2 // coils
    line = [jnp.sum(offsets[row : row + 1, tap : tap + 1]) for tap in range(taps)]
    chunks = value.shape[1] // LANES
    for i in range(chunks):
        state[i] = value[:, i * LANES : (i + 1) * LANES]
        for part in range(2):
            for tap in range(taps):
                source = pl.ds(part * coils * lines + line[tap], coils, stride=lines)
                picked[i, pl.ds(part * coils * taps + tap, coils, stride=taps), :] = state[i, source, :]
    return jnp.concatenate([picked[i] for i in range(chunks)], axis=1)


def pick_scratch(lanes, state, size):
    return [pltpu.VMEM((lanes // LANES, state, LANES), F32), pltpu.VMEM((lanes // LANES, size, LANES), F32)]


def visits(segs, backward):
    if backward:
        return [(s, segs + s - 1 if s else 2 * segs + 1) for s in reversed(range(segs))]
    return [(s, s + 1 if s < segs - 1 else 2 * segs) for s in range(segs)]


def walk(maps, carried, sources, choose, backward, sends):
    states = list(sources)
    order = visits(len(sources), backward)
    for s, row in order:
        if carried is not None:
            states[s] = product(maps(s), carried) + sources[s]
        if sends or s != order[-1][0]:
            carried = choose(states[s], row=row)
    return carried if sends else states


def response(high, low, states, choose, backward):
    size = high.shape[2]
    first = visits(len(states), backward)[0][0]
    columns = high[first, :, : size // 2].astype(F32) + low[first, :, : size // 2].astype(F32)
    blank = jnp.zeros_like(columns)
    sources = [jnp.concatenate([columns if s == first else blank, state], axis=1) for s, state in enumerate(states)]
    return walk(lambda s: (high[s], low[s]), None, sources, choose, backward, True)


def spot(near, i):
    return lax.bitwise_xor(lax.axis_index("coil"), i) if near else i


def my_chip():
    seg = lax.axis_index("seg")
    return lax.shift_right_logical(seg, 1), lax.bitwise_and(seg, 1)


def pack(measured):
    segs, parts, coils, lines, samples = measured.shape
    n = lax.axis_size("coil")
    width = samples // n

    def body(m_ref, *rest):
        outs, sems = rest[:n], rest[n]
        copies = []
        for i in range(n):
            start = pl.multiple_of(spot(True, i) * width, width)
            copies.append(pltpu.make_async_copy(m_ref.at[:, :, :, :, pl.ds(start, width)], outs[i], sems.at[i]))
        for c in copies:
            c.start()
        for c in copies:
            c.wait()

    out = ((segs, parts, coils, lines, width), F32)
    return call(body, "pack", [out] * n, [HBM], [pltpu.SemaphoreType.DMA((n,))])(measured)


def hold(first, *values):
    def body(_, *refs):
        for i in range(len(values)):
            refs[len(values) + i][...] = refs[i][...]

    out_shape = [(v.shape, v.dtype) for v in values]
    return call(body, "hold", out_shape, [ANY] + [VMEM] * len(values))(first, *values)


def gather(near, blocks, after):
    n = len(blocks)
    segs, parts, coils, lines, width = blocks[0].shape

    def body(*refs):
        for i in range(n):
            refs[n][:, :, pl.ds(spot(near, i) * coils, coils)] = refs[i][...]

    out = ((segs, parts, n * coils, lines, width), F32)
    return call(body, "gather", [out], [VMEM] * n, after=after)(*blocks)[0]


def prepare(near, blocks, backward):
    n = len(blocks)
    segs, _, block_cols, rows = blocks[0].shape
    cols = block_cols * n
    size = 2 * cols

    def body(*refs):
        hi_ref, lo_ref, kt = refs[n:]
        for i in range(n):
            kt[:, :, pl.ds(spot(near, i), 1)] = refs[i][...][:, :, None]
        for s in range(segs):
            real, imag = (kt[s, part].reshape(cols, rows).T for part in range(2))
            hi_ref[s], lo_ref[s] = halves(real_form(jnp.concatenate([real, imag], axis=0)))

    return call(
        body,
        "prepare_backward" if backward else "prepare_forward",
        [((segs, 2 * rows, size), BF16)] * 2,
        [VMEM] * n,
        [pltpu.VMEM((segs, 2, n, block_cols, rows), F32)],
    )(*blocks)


def summary(offsets, maps, sources, backward):
    high, low = maps
    _, rows, size = high.shape
    segs, _, coils, _, width = sources.shape
    lanes = size // 2 + width

    def body(off_ref, hi_ref, lo_ref, m_ref, e_ref, state, picked):
        choose = functools.partial(pick, state=state, picked=picked, offsets=off_ref, coils=coils)
        e_ref[...] = response(hi_ref, lo_ref, [m_ref[s].reshape(rows, width) for s in range(segs)], choose, backward)

    return call(
        body,
        "summary_backward" if backward else "summary_forward",
        [((size, lanes), F32)],
        [VMEM] * 4,
        pick_scratch(lanes, rows, size),
    )(offsets, high, low, sources)[0]


def compose(mine, other, cols, backward):
    size, lanes = mine.shape

    def body(a_ref, b_ref, whole, out_ref):
        _, core = my_chip()
        leads = core == (1 if backward else 0)
        near = jnp.where(leads, a_ref[...], b_ref[...])
        far = jnp.where(leads, b_ref[...], a_ref[...])
        both = product(halves(real_form(far[:, :cols])), near)
        whole[:, :cols] = both[:, :cols]
        whole[:, cols:] = both[:, cols:] + far[:, cols:]
        out_ref[...] = whole[pl.ds(pl.multiple_of(core * (size // 2), size // 2), size // 2), :]

    return call(
        body,
        "compose_backward" if backward else "compose_forward",
        [((size, lanes), F32), ((size // 2, lanes), F32)],
        [VMEM, VMEM],
    )(mine, other)


def incoming(own, parts, table, carried, backward):
    chips, _, cols, _ = table.shape
    chip, core = my_chip()
    table[pl.ds(chip, 1)] = own[...].reshape((1,) + table.shape[1:])
    for i in range(1, chips):
        e = lax.bitwise_xor(chip, i)
        table[pl.ds(e, 1), pl.ds(core, 1)] = parts[2 * i - 2][...][None, None]
        table[pl.ds(e, 1), pl.ds(1 - core, 1)] = parts[2 * i - 1][...][None, None]
    order = list(range(chips))[:: -1 if backward else 1]
    carried[order[0]] = jnp.zeros(carried.shape[1:], F32)
    value = None
    for at, e in enumerate(order[:-1]):
        block = table[e].reshape(2 * cols, -1)
        if value is None:
            value = block[:, cols:]
        else:
            value = product(halves(real_form(block[:, :cols])), value) + block[:, cols:]
        carried[order[at + 1]] = value
    return carried[chip]


def incoming_scratch(chips, size, lanes):
    return [pltpu.VMEM((chips, 2, size // 2, lanes), F32), pltpu.VMEM((chips, size, lanes - size // 2), F32)]


def finish(near, offsets, maps, sources, mine, other, blocks, backward, joined=None, after=()):
    high, low = maps
    segs, _, coils, lines, width = sources.shape
    _, rows, size = high.shape
    cols, lanes = size // 2, mine.shape[1]
    chips = (len(blocks) + 1) // 2
    n = lax.axis_size("coil")
    own_coils = coils // n
    extra = [] if joined is None else [joined]

    def body(off_ref, hi_ref, lo_ref, m_ref, a_ref, b_ref, own, *refs):
        at = 2 * chips - 2
        rest, extra_refs, refs = refs[:at], refs[at : at + len(extra)], refs[at + len(extra) :]
        pieces = n if backward else 0
        outs, refs = refs[:pieces], refs[pieces:]
        whole, table, carried, state, picked = refs
        choose = functools.partial(pick, state=state, picked=picked, offsets=off_ref, coils=coils)
        value = incoming(own, rest, table, carried, backward)
        moved = product(halves(real_form(b_ref[:, :cols])), value) + b_ref[:, cols:]
        value = jnp.where(my_chip()[1] == (1 if backward else 0), value, moved)
        source = [m_ref[s].reshape(rows, width) for s in range(segs)]
        states = walk(lambda s: (hi_ref[s], lo_ref[s]), value, source, choose, backward, False)
        for s in range(segs):
            whole[s] = states[s].reshape(2, coils, lines, width)
        for i in range(len(outs)):
            cut = whole[:, :, pl.ds(spot(near, i) * own_coils, own_coils)]
            if joined is not None and i == 1:
                outs[i][0] = extra_refs[-1][...]
                outs[i][1] = cut
            else:
                outs[i][...] = cut

    block = (segs, 2, own_coils, lines, width)
    out_shape = [((2, *block) if joined is not None and i == 1 else block, F32) for i in range(n)]
    scratch = [pltpu.VMEM(sources.shape, F32)]
    if not backward:
        out_shape = [(sources.shape, F32)]
        scratch = []
    return call(
        body,
        "finish_backward" if backward else "finish_forward",
        out_shape,
        [VMEM] * (6 + len(blocks) + len(extra)),
        scratch + incoming_scratch(chips, size, lanes) + pick_scratch(width, rows, size),
        after=after,
    )(offsets, high, low, sources, mine, other, *blocks, *extra)


def cut(near, states, n, after):
    segs, parts, coils, lines, width = states.shape
    own_coils = coils // n

    def body(s_ref, *outs):
        for i in range(n):
            outs[i][...] = s_ref[:, :, pl.ds(spot(near, i) * own_coils, own_coils)]

    out = ((segs, parts, own_coils, lines, width), F32)
    return call(body, "cut", [out] * n, [VMEM], after=after)(states)


def unpack(blocks, begun=()):
    n = lax.axis_size("coil")
    arrays, places = [], []
    for i, pair in blocks:
        for o in range(2):
            if isinstance(pair, tuple):
                if pair[o] is None:
                    continue
                places.append((len(arrays), i, o, False))
                arrays.append(pair[o])
            else:
                places.append((len(arrays), i, o, True))
        if not isinstance(pair, tuple):
            arrays.append(pair)
    segs, parts, coils, lines, width = arrays[0].shape[-5:]

    def body(*refs):
        ins, outs, sems = refs[len(begun) :], refs[len(begun) + len(arrays) :], refs[-1]
        copies = []
        for k, (at, i, o, joined) in enumerate(places):
            start = pl.multiple_of(spot(True, i) * width, width)
            source = ins[at].at[o] if joined else ins[at]
            copies.append(pltpu.make_async_copy(source, outs[o].at[:, :, :, :, pl.ds(start, width)], sems.at[k]))
        for c in copies:
            c.start()
        for c in copies:
            c.wait()

    return call(
        body,
        "unpack_rest" if begun else "unpack",
        [((segs, parts, coils, lines, n * width), F32)] * 2,
        [ANY] * len(begun) + [VMEM] * len(arrays),
        [pltpu.SemaphoreType.DMA((len(places),))],
        [ANY] * 2,
        aliases={i: i for i in range(len(begun))},
    )(*begun, *arrays)


def swap(block, axis, distance):
    return lax.ppermute(block, axis, [(i, i ^ distance) for i in range(lax.axis_size(axis))])


def spread_kernels(own):
    n = lax.axis_size("coil")
    blocks = {0: own}
    distance = n // 2
    while distance:
        blocks.update({i ^ distance: swap(blocks[i], "coil", distance) for i in sorted(blocks)})
        distance //= 2
    return [blocks[i] for i in range(n)]


def exchange(whole, half, first=None):
    chips = lax.axis_size("seg") // 2
    blocks = [whole]
    for i in range(1, chips):
        block = swap(half, "seg", 2 * i)
        if i == min(2, chips - 1) and first is not None:
            (block,) = hold(first, block)
        blocks += [block, swap(block, "seg", 1)]
    return blocks


def shards(measured, forward_kernel, backward_kernel, line_offsets):
    n = lax.axis_size("coil")
    places = lax.axis_size("seg")
    taps = line_offsets.shape[2]
    width = measured.shape[4] // n
    cols = forward_kernel.shape[3] * n
    kernels_f, kernels_b = (jnp.swapaxes(k, 2, 3) for k in (forward_kernel, backward_kernel))
    aligned = width % LANES == 0 and (cols // taps // n) % 8 == 0
    if aligned:
        forward_blocks = spread_kernels(kernels_f)
        backward_blocks = spread_kernels(kernels_b)
        pieces = pack(measured)
        lines_blocks = [pieces[0]] + [swap(pieces[i], "coil", i) for i in range(1, n)]
    else:
        forward_blocks = list(lax.all_gather(kernels_f, "coil"))
        backward_blocks = list(lax.all_gather(kernels_b, "coil"))
        split = lax.all_to_all(measured, "coil", split_axis=4, concat_axis=2, tiled=True)
        split = jnp.pad(split, [(0, 0)] * 4 + [(0, -width % LANES)])
        lines_blocks = jnp.split(split, n, axis=2)
    after = lax.ppermute(line_offsets[0, 0], "seg", [((i + 1) % places, i) for i in range(places)])[None]
    before = lax.ppermute(line_offsets[-1, 1], "seg", [(i, (i + 1) % places) for i in range(places)])[None]
    offsets = jnp.concatenate([line_offsets[:, 0], line_offsets[:, 1], after, before])
    offsets = jnp.pad(offsets, [(0, -offsets.shape[0] % 8), (0, LANES - taps)])

    forward_maps = prepare(aligned, forward_blocks, False)
    lines = gather(aligned, lines_blocks, forward_maps[:1])
    backward_maps = prepare(aligned, backward_blocks, True)
    mine = summary(offsets, forward_maps, lines, False)
    other = swap(mine, "seg", 1)
    blocks = exchange(*compose(mine, other, cols, False))
    (forward,) = finish(aligned, offsets, forward_maps, lines, mine, other, blocks, False)
    forward_out = cut(aligned, forward, n, backward_maps[:1])
    mine = summary(offsets, backward_maps, forward, True)
    other = swap(mine, "seg", 1)
    whole, half = compose(mine, other, cols, True)
    if aligned:
        home = dict(enumerate(forward_out[:2])) | {i: swap(forward_out[i], "coil", i) for i in range(2, n)}
        blocks = exchange(whole, half, home[n - 1] if n > 2 else None)
        result_out = finish(
            aligned,
            offsets,
            backward_maps,
            forward,
            mine,
            other,
            blocks,
            True,
            joined=forward_out[1],
            after=[home[i] for i in range(2, n - 1)],
        )
        result_home = [result_out[0]] + [swap(result_out[i], "coil", i) for i in range(1, n)]
        begun = unpack([(0, (home[0], result_out[0]))] + [(i, (home[i], None)) for i in range(2, n)])
        for i in range(1, n):
            begun = unpack([(i, (None, result_home[i]) if i > 1 else result_home[i])], begun)
        return tuple(begun)
    blocks = exchange(whole, half)
    result_out = finish(aligned, offsets, backward_maps, forward, mine, other, blocks, True)

    def rejoin(blocks):
        states = lax.all_to_all(jnp.stack(blocks), "coil", split_axis=0, concat_axis=0)[..., :width]
        states = jnp.moveaxis(states, 0, 4)
        return states.reshape(states.shape[:4] + (n * width,))

    return rejoin(forward_out), rejoin(result_out)


def solution(mesh):
    placed = (
        P("seg", None, "coil", None, None),
        P("seg", None, None, "coil"),
        P("seg", None, None, "coil"),
        P("seg", None, None),
    )
    return jax.shard_map(
        shards,
        mesh=mesh,
        in_specs=placed,
        out_specs=(P("seg", None, "coil", None, None), P("seg", None, "coil", None, None)),
        check_vma=False,
    )
```

```python
import functools

import jax
import jax.numpy as jnp
from jax import lax
from jax.experimental import pallas as pl
from jax.experimental.pallas import tpu as pltpu
from jax.sharding import PartitionSpec as P

F32 = jnp.float32
BF16 = jnp.bfloat16
VMEM = pl.BlockSpec(memory_space=pltpu.VMEM)
ANY = pl.BlockSpec(memory_space=pl.ANY)
HBM = pl.BlockSpec(memory_space=pltpu.HBM)
LANES = 128
PARAMS = pltpu.CompilerParams(vmem_limit_bytes=40 * 2**20)


def call(body, name, out_shape, in_specs, scratch=(), out_specs=None, after=(), aliases=None):
    def whole(*refs):
        body(*refs[len(after) :])

    kernel = pl.pallas_call(
        whole,
        out_shape=[jax.ShapeDtypeStruct(shape, dtype) for shape, dtype in out_shape],
        in_specs=[ANY] * len(after) + in_specs,
        out_specs=out_specs or [VMEM] * len(out_shape),
        scratch_shapes=list(scratch),
        input_output_aliases=aliases or {},
        compiler_params=PARAMS,
        name=name,
    )
    return functools.partial(kernel, *after)


def halves(a):
    high = a.astype(BF16)
    return high, (a - high.astype(F32)).astype(BF16)


def product(left, right):
    dot = functools.partial(jnp.dot, preferred_element_type=F32)
    high, low = left
    other_high, other_low = halves(right)
    width = right.shape[1]
    if width > LANES:
        return dot(high, other_high) + (dot(high, other_low) + dot(low, other_high))
    both = dot(high, jnp.concatenate([other_high, other_low], axis=1))
    return both[:, :width] + (both[:, width:] + dot(low, other_high))


def real_form(columns):
    size = columns.shape[0] // 2
    return jnp.concatenate([columns, jnp.concatenate([-columns[size:], columns[:size]], axis=0)], axis=1)


def pick(value, state, picked, offsets, coils, row):
    taps, lines = picked.shape[1] // 2 // coils, state.shape[1] // 2 // coils
    line = [jnp.sum(offsets[row : row + 1, tap : tap + 1]) for tap in range(taps)]
    chunks = value.shape[1] // LANES
    for i in range(chunks):
        state[i] = value[:, i * LANES : (i + 1) * LANES]
        for part in range(2):
            for tap in range(taps):
                source = pl.ds(part * coils * lines + line[tap], coils, stride=lines)
                picked[i, pl.ds(part * coils * taps + tap, coils, stride=taps), :] = state[i, source, :]
    return jnp.concatenate([picked[i] for i in range(chunks)], axis=1)


def pick_scratch(lanes, state, size):
    return [pltpu.VMEM((lanes // LANES, state, LANES), F32), pltpu.VMEM((lanes // LANES, size, LANES), F32)]


def visits(segs, backward):
    if backward:
        return [(s, segs + s - 1 if s else 2 * segs + 1) for s in reversed(range(segs))]
    return [(s, s + 1 if s < segs - 1 else 2 * segs) for s in range(segs)]


def walk(maps, carried, sources, choose, backward, sends):
    states = list(sources)
    order = visits(len(sources), backward)
    for s, row in order:
        if carried is not None:
            states[s] = product(maps(s), carried) + sources[s]
        if sends or s != order[-1][0]:
            carried = choose(states[s], row=row)
    return carried if sends else states


def response(high, low, states, choose, backward):
    size = high.shape[2]
    first = visits(len(states), backward)[0][0]
    columns = high[first, :, : size // 2].astype(F32) + low[first, :, : size // 2].astype(F32)
    blank = jnp.zeros_like(columns)
    sources = [jnp.concatenate([columns if s == first else blank, state], axis=1) for s, state in enumerate(states)]
    return walk(lambda s: (high[s], low[s]), None, sources, choose, backward, True)


def spot(near, i):
    return lax.bitwise_xor(lax.axis_index("coil"), i) if near else i


def my_chip():
    seg = lax.axis_index("seg")
    return lax.shift_right_logical(seg, 1), lax.bitwise_and(seg, 1)


def pack(measured):
    segs, parts, coils, lines, samples = measured.shape
    n = lax.axis_size("coil")
    width = samples // n

    def body(m_ref, *rest):
        outs, sems = rest[:n], rest[n]
        copies = []
        for i in range(n):
            start = pl.multiple_of(spot(True, i) * width, width)
            copies.append(pltpu.make_async_copy(m_ref.at[:, :, :, :, pl.ds(start, width)], outs[i], sems.at[i]))
        for c in copies:
            c.start()
        for c in copies:
            c.wait()

    out = ((segs, parts, coils, lines, width), F32)
    return call(body, "pack", [out] * n, [HBM], [pltpu.SemaphoreType.DMA((n,))])(measured)


def hold(first, *values):
    def body(_, *refs):
        for i in range(len(values)):
            refs[len(values) + i][...] = refs[i][...]

    out_shape = [(v.shape, v.dtype) for v in values]
    return call(body, "hold", out_shape, [ANY] + [VMEM] * len(values))(first, *values)


def gather(near, blocks, after):
    n = len(blocks)
    segs, parts, coils, lines, width = blocks[0].shape

    def body(*refs):
        for i in range(n):
            refs[n][:, :, pl.ds(spot(near, i) * coils, coils)] = refs[i][...]

    out = ((segs, parts, n * coils, lines, width), F32)
    return call(body, "gather", [out], [VMEM] * n, after=after)(*blocks)[0]


def prepare(near, blocks, backward):
    n = len(blocks)
    segs, _, block_cols, rows = blocks[0].shape
    cols = block_cols * n
    size = 2 * cols

    def body(*refs):
        hi_ref, lo_ref, kt = refs[n:]
        for i in range(n):
            kt[:, :, pl.ds(spot(near, i), 1)] = refs[i][...][:, :, None]
        for s in range(segs):
            real, imag = (kt[s, part].reshape(cols, rows).T for part in range(2))
            hi_ref[s], lo_ref[s] = halves(real_form(jnp.concatenate([real, imag], axis=0)))

    return call(
        body,
        "prepare_backward" if backward else "prepare_forward",
        [((segs, 2 * rows, size), BF16)] * 2,
        [VMEM] * n,
        [pltpu.VMEM((segs, 2, n, block_cols, rows), F32)],
    )(*blocks)


def summary(offsets, maps, sources, backward):
    high, low = maps
    _, rows, size = high.shape
    segs, _, coils, _, width = sources.shape
    lanes = size // 2 + width

    def body(off_ref, hi_ref, lo_ref, m_ref, e_ref, state, picked):
        choose = functools.partial(pick, state=state, picked=picked, offsets=off_ref, coils=coils)
        e_ref[...] = response(hi_ref, lo_ref, [m_ref[s].reshape(rows, width) for s in range(segs)], choose, backward)

    return call(
        body,
        "summary_backward" if backward else "summary_forward",
        [((size, lanes), F32)],
        [VMEM] * 4,
        pick_scratch(lanes, rows, size),
    )(offsets, high, low, sources)[0]


def compose(mine, other, cols, backward):
    size, lanes = mine.shape

    def body(a_ref, b_ref, whole, out_ref):
        _, core = my_chip()
        leads = core == (1 if backward else 0)
        near = jnp.where(leads, a_ref[...], b_ref[...])
        far = jnp.where(leads, b_ref[...], a_ref[...])
        both = product(halves(real_form(far[:, :cols])), near)
        whole[:, :cols] = both[:, :cols]
        whole[:, cols:] = both[:, cols:] + far[:, cols:]
        out_ref[...] = whole[pl.ds(pl.multiple_of(core * (size // 2), size // 2), size // 2), :]

    return call(
        body,
        "compose_backward" if backward else "compose_forward",
        [((size, lanes), F32), ((size // 2, lanes), F32)],
        [VMEM, VMEM],
    )(mine, other)


def incoming(own, parts, table, carried, backward):
    chips, _, cols, _ = table.shape
    chip, core = my_chip()
    table[pl.ds(chip, 1)] = own[...].reshape((1,) + table.shape[1:])
    for i in range(1, chips):
        e = lax.bitwise_xor(chip, i)
        table[pl.ds(e, 1), pl.ds(core, 1)] = parts[2 * i - 2][...][None, None]
        table[pl.ds(e, 1), pl.ds(1 - core, 1)] = parts[2 * i - 1][...][None, None]
    order = list(range(chips))[:: -1 if backward else 1]
    carried[order[0]] = jnp.zeros(carried.shape[1:], F32)
    value = None
    for at, e in enumerate(order[:-1]):
        block = table[e].reshape(2 * cols, -1)
        if value is None:
            value = block[:, cols:]
        else:
            value = product(halves(real_form(block[:, :cols])), value) + block[:, cols:]
        carried[order[at + 1]] = value
    return carried[chip]


def incoming_scratch(chips, size, lanes):
    return [pltpu.VMEM((chips, 2, size // 2, lanes), F32), pltpu.VMEM((chips, size, lanes - size // 2), F32)]


def finish(near, offsets, maps, sources, mine, other, blocks, backward, joined=None, after=()):
    high, low = maps
    segs, _, coils, lines, width = sources.shape
    _, rows, size = high.shape
    cols, lanes = size // 2, mine.shape[1]
    chips = (len(blocks) + 1) // 2
    n = lax.axis_size("coil")
    own_coils = coils // n
    extra = [] if joined is None else [joined]

    def body(off_ref, hi_ref, lo_ref, m_ref, a_ref, b_ref, own, *refs):
        at = 2 * chips - 2
        rest, extra_refs, refs = refs[:at], refs[at : at + len(extra)], refs[at + len(extra) :]
        pieces = n if backward else 0
        outs, refs = refs[:pieces], refs[pieces:]
        whole, table, carried, state, picked = refs
        choose = functools.partial(pick, state=state, picked=picked, offsets=off_ref, coils=coils)
        value = incoming(own, rest, table, carried, backward)
        moved = product(halves(real_form(b_ref[:, :cols])), value) + b_ref[:, cols:]
        value = jnp.where(my_chip()[1] == (1 if backward else 0), value, moved)
        source = [m_ref[s].reshape(rows, width) for s in range(segs)]
        states = walk(lambda s: (hi_ref[s], lo_ref[s]), value, source, choose, backward, False)
        for s in range(segs):
            whole[s] = states[s].reshape(2, coils, lines, width)
        for i in range(len(outs)):
            cut = whole[:, :, pl.ds(spot(near, i) * own_coils, own_coils)]
            if joined is not None and i == 1:
                outs[i][0] = extra_refs[-1][...]
                outs[i][1] = cut
            else:
                outs[i][...] = cut

    block = (segs, 2, own_coils, lines, width)
    out_shape = [((2, *block) if joined is not None and i == 1 else block, F32) for i in range(n)]
    scratch = [pltpu.VMEM(sources.shape, F32)]
    if not backward:
        out_shape = [(sources.shape, F32)]
        scratch = []
    return call(
        body,
        "finish_backward" if backward else "finish_forward",
        out_shape,
        [VMEM] * (6 + len(blocks) + len(extra)),
        scratch + incoming_scratch(chips, size, lanes) + pick_scratch(width, rows, size),
        after=after,
    )(offsets, high, low, sources, mine, other, *blocks, *extra)


def cut(near, states, n, after):
    segs, parts, coils, lines, width = states.shape
    own_coils = coils // n

    def body(s_ref, *outs):
        for i in range(n):
            outs[i][...] = s_ref[:, :, pl.ds(spot(near, i) * own_coils, own_coils)]

    out = ((segs, parts, own_coils, lines, width), F32)
    return call(body, "cut", [out] * n, [VMEM], after=after)(states)


def unpack(blocks, begun=()):
    n = lax.axis_size("coil")
    arrays, places = [], []
    for i, pair in blocks:
        for o in range(2):
            if isinstance(pair, tuple):
                if pair[o] is None:
                    continue
                places.append((len(arrays), i, o, False))
                arrays.append(pair[o])
            else:
                places.append((len(arrays), i, o, True))
        if not isinstance(pair, tuple):
            arrays.append(pair)
    segs, parts, coils, lines, width = arrays[0].shape[-5:]

    def body(*refs):
        ins, outs, sems = refs[len(begun) :], refs[len(begun) + len(arrays) :], refs[-1]
        copies = []
        for k, (at, i, o, joined) in enumerate(places):
            start = pl.multiple_of(spot(True, i) * width, width)
            source = ins[at].at[o] if joined else ins[at]
            copies.append(pltpu.make_async_copy(source, outs[o].at[:, :, :, :, pl.ds(start, width)], sems.at[k]))
        for c in copies:
            c.start()
        for c in copies:
            c.wait()

    return call(
        body,
        "unpack_rest" if begun else "unpack",
        [((segs, parts, coils, lines, n * width), F32)] * 2,
        [ANY] * len(begun) + [VMEM] * len(arrays),
        [pltpu.SemaphoreType.DMA((len(places),))],
        [ANY] * 2,
        aliases={i: i for i in range(len(begun))},
    )(*begun, *arrays)


def swap(block, axis, distance):
    return lax.ppermute(block, axis, [(i, i ^ distance) for i in range(lax.axis_size(axis))])


def spread_kernels(own):
    n = lax.axis_size("coil")
    blocks = {0: own}
    distance = n // 2
    while distance:
        blocks.update({i ^ distance: swap(blocks[i], "coil", distance) for i in sorted(blocks)})
        distance //= 2
    return [blocks[i] for i in range(n)]


def exchange(whole, half, first=None):
    chips = lax.axis_size("seg") // 2
    blocks = [whole]
    for i in range(1, chips):
        block = swap(half, "seg", 2 * i)
        if i == min(3, chips - 1) and first is not None:
            (block,) = hold(first, block)
        blocks += [block, swap(block, "seg", 1)]
    return blocks


def shards(measured, forward_kernel, backward_kernel, line_offsets):
    n = lax.axis_size("coil")
    places = lax.axis_size("seg")
    taps = line_offsets.shape[2]
    width = measured.shape[4] // n
    cols = forward_kernel.shape[3] * n
    kernels_f, kernels_b = (jnp.swapaxes(k, 2, 3) for k in (forward_kernel, backward_kernel))
    aligned = width % LANES == 0 and (cols // taps // n) % 8 == 0
    if aligned:
        forward_blocks = spread_kernels(kernels_f)
        backward_blocks = spread_kernels(kernels_b)
        pieces = pack(measured)
        lines_blocks = [pieces[0]] + [swap(pieces[i], "coil", i) for i in range(1, n)]
    else:
        forward_blocks = list(lax.all_gather(kernels_f, "coil"))
        backward_blocks = list(lax.all_gather(kernels_b, "coil"))
        split = lax.all_to_all(measured, "coil", split_axis=4, concat_axis=2, tiled=True)
        split = jnp.pad(split, [(0, 0)] * 4 + [(0, -width % LANES)])
        lines_blocks = jnp.split(split, n, axis=2)
    after = lax.ppermute(line_offsets[0, 0], "seg", [((i + 1) % places, i) for i in range(places)])[None]
    before = lax.ppermute(line_offsets[-1, 1], "seg", [(i, (i + 1) % places) for i in range(places)])[None]
    offsets = jnp.concatenate([line_offsets[:, 0], line_offsets[:, 1], after, before])
    offsets = jnp.pad(offsets, [(0, -offsets.shape[0] % 8), (0, LANES - taps)])

    forward_maps = prepare(aligned, forward_blocks, False)
    lines = gather(aligned, lines_blocks, forward_maps[:1])
    backward_maps = prepare(aligned, backward_blocks, True)
    mine = summary(offsets, forward_maps, lines, False)
    other = swap(mine, "seg", 1)
    blocks = exchange(*compose(mine, other, cols, False))
    (forward,) = finish(aligned, offsets, forward_maps, lines, mine, other, blocks, False)
    forward_out = cut(aligned, forward, n, backward_maps[:1])
    mine = summary(offsets, backward_maps, forward, True)
    other = swap(mine, "seg", 1)
    whole, half = compose(mine, other, cols, True)
    if aligned:
        home = dict(enumerate(forward_out[:2])) | {i: swap(forward_out[i], "coil", i) for i in range(2, n)}
        blocks = exchange(whole, half, home[n - 1] if n > 2 else None)
        result_out = finish(
            aligned,
            offsets,
            backward_maps,
            forward,
            mine,
            other,
            blocks,
            True,
            joined=forward_out[1],
            after=[home[i] for i in range(2, n - 1)],
        )
        result_home = [result_out[0]] + [swap(result_out[i], "coil", i) for i in range(1, n)]
        begun = unpack([(0, (home[0], result_out[0]))] + [(i, (home[i], None)) for i in range(2, n)])
        for i in range(1, n):
            begun = unpack([(i, (None, result_home[i]) if i > 1 else result_home[i])], begun)
        return tuple(begun)
    blocks = exchange(whole, half)
    result_out = finish(aligned, offsets, backward_maps, forward, mine, other, blocks, True)

    def rejoin(blocks):
        states = lax.all_to_all(jnp.stack(blocks), "coil", split_axis=0, concat_axis=0)[..., :width]
        states = jnp.moveaxis(states, 0, 4)
        return states.reshape(states.shape[:4] + (n * width,))

    return rejoin(forward_out), rejoin(result_out)


def solution(mesh):
    placed = (
        P("seg", None, "coil", None, None),
        P("seg", None, None, "coil"),
        P("seg", None, None, "coil"),
        P("seg", None, None),
    )
    return jax.shard_map(
        shards,
        mesh=mesh,
        in_specs=placed,
        out_specs=(P("seg", None, "coil", None, None), P("seg", None, "coil", None, None)),
        check_vma=False,
    )
```
